256 devices in a mesh: lat: 16 (over x, y_lo, core), lon: 16 (over z, y_hi).
Axes of the slice: x: 4, y: 4 (y_hi: 2, y_lo: 2; y = y_hi * 2 + y_lo), z: 8, core: 2. Of those that a mesh axis runs over, the one named last changes fastest.
Arguments:
- features: bfloat16 [256, 1440, 256], P('lat', 'lon'), may hold values from -6 to 6
- cotangent: bfloat16 [256, 1440, 256], P('lat', 'lon'), may hold values from -6 to 6
- basis: bfloat16 [256, 3, 3, 33], P('lat'), may hold values from -0.625 to 0.625
- support: int32 [256], P('lat'), may hold values from 1 to 16, as said below
- weight_one: bfloat16 [3, 256, 256], replicated, may hold values from -0.21875 to 0.21875
- weight_two: bfloat16 [3, 256, 256], replicated, may hold values from -0.21875 to 0.21875
Outputs:
- layer_out: bfloat16 [256, 1440, 256], P('lat', 'lon')
- grad_input: bfloat16 [256, 1440, 256], P('lat', 'lon')
- grad_one: float32 [3, 256, 256], replicated
- grad_two: float32 [3, 256, 256], replicated
The draws below stay inside these ranges and needn't reach their ends.
Inputs may be any that keep to these rules, and one draw needn't show every extreme that they name: support[r] is how many cells on each side along longitude the filter of row r reaches; the first and the last row reach 16.
All inputs are finite; a program needn't handle non-finite values.
Results may differ from the reference program's by a relative error of at most 0.006.
The reference program's roundings to bfloat16 on the way (of `filtered`, `y_one`, `hidden`, `y_two`, `dy_two`, `dz_one` and `dy_one`) count: a program that leaves them out, or rounds other values in their place, can miss the bound.
Values may be sent and summed in bfloat16 or wider, within the bound.
A program may use at most 64 MiB of HBM per device.

```python
import math
import jax
import jax.numpy as jnp
from jax import lax

C = 256
K = 3
HW = 16
SPAN = 33
NLAT = 256
NLON = 1440


def draw_support(key, part):
    key = jax.random.fold_in(key, 7)
    row_idx = jnp.arange(NLAT, dtype=jnp.int32)
    pole_dist = jnp.minimum(row_idx, NLAT - 1 - row_idx)
    half_rows = max(NLAT // 2, 1)
    base_width = HW - pole_dist * HW // half_rows
    jitter = jax.random.randint(key, (NLAT,), -2, 3, dtype=jnp.int32)
    reach = jnp.clip(base_width + jitter, 1, HW)
    return jnp.where(pole_dist == 0, HW, reach).astype(jnp.int32)


def shard_levels(rng, shape, cuts, low, largest):
    def one(dim, shards_of):
        steps = jax.random.uniform(jax.random.fold_in(jax.random.fold_in(rng, 6), dim), (shards_of,), jnp.float32, low / len(cuts), largest / len(cuts))
        return jnp.repeat(jnp.exp(steps), shape[dim] // shards_of).reshape((-1,) + (1,) * (len(shape) - dim - 1))

    factor_of = one(*cuts[0])
    for cut in cuts[1:]:
        factor_of = factor_of * one(*cut)
    return factor_of


def bell_draw(rng, extent, deviation, bound, cuts=(), kind=jnp.bfloat16):
    array = jax.random.normal(rng, extent, jnp.float32) * deviation
    if len(cuts) > 0:
        array = shard_levels(rng, extent, cuts, -0.22, 0.18) * array
    return jnp.clip(array, min=-bound, max=bound).astype(kind)


def setup_inputs(seed: int = 0) -> dict:
    keys = jax.random.split(jax.random.key(seed), 7)
    return {
        "features": bell_draw(keys[0], (NLAT, NLON, C), 1.0, 6.0, ((0, 16), (1, 16))),
        "cotangent": bell_draw(keys[1], (NLAT, NLON, C), 1.0, 6.0, ((0, 16), (1, 16))),
        "basis": bell_draw(keys[2], (NLAT, K, 3, SPAN), (3 * SPAN) ** -0.5, 0.625, ((0, 16),)),
        "support": draw_support(jax.random.fold_in(keys[6], 71), 0),
        "weight_one": bell_draw(keys[4], (K, C, C), (K * C) ** -0.5, 0.21875),
        "weight_two": bell_draw(keys[5], (K, C, C), (K * C) ** -0.5, 0.21875),
    }


def mask_filter(basis, support):
    offset = jnp.abs(jnp.arange(SPAN, dtype=jnp.int32) - HW)
    inside = offset[None, :] <= support[:, None]
    return jnp.where(inside[:, None, None, :], basis, jnp.zeros_like(basis))

def lon_wrap(field):
    return jnp.concatenate([field[:, NLON - HW:], field, field[:, :HW]], axis=1)

def stencil(field, filtered):
    padded = jnp.pad(lon_wrap(field), ((1, 1), (0, 0), (0, 0)))

    def one_row(row_idx):
        band_rows = lax.dynamic_slice_in_dim(padded, row_idx, 3, 0).astype(jnp.float32)
        weights_row = lax.dynamic_index_in_dim(filtered, row_idx, 0, keepdims=False).astype(jnp.float32)

        def add_offset(offset_idx, total):
            window = lax.dynamic_slice_in_dim(band_rows, offset_idx, NLON, 1)
            factor = lax.dynamic_index_in_dim(weights_row, offset_idx, 2, keepdims=False)
            return total + jnp.einsum('ka,ajc->jkc', factor, window)
        total = lax.fori_loop(0, SPAN, add_offset, jnp.zeros((NLON, K, C), jnp.float32))
        return total.astype(jnp.bfloat16)
    return lax.map(one_row, jnp.arange(NLAT, dtype=jnp.int32))

def transposed(grad_field, filtered):
    padded = jnp.pad(lon_wrap(grad_field), ((1, 1), (0, 0), (0, 0), (0, 0)))
    filter_pad = jnp.pad(filtered, ((1, 1), (0, 0), (0, 0), (0, 0)))
    three_idx = jnp.arange(3, dtype=jnp.int32)

    def one_row(row_idx):
        band_rows = lax.dynamic_slice_in_dim(padded, row_idx, 3, 0).astype(jnp.float32)
        weights_rows = lax.dynamic_slice_in_dim(filter_pad, row_idx, 3, 0).astype(jnp.float32)
        picked = weights_rows[three_idx, :, 2 - three_idx, :]

        def add_offset(offset_idx, total):
            window = lax.dynamic_slice_in_dim(band_rows, 2 * HW - offset_idx, NLON, 1)
            factor = lax.dynamic_index_in_dim(picked, offset_idx, 2, keepdims=False)
            return total + jnp.einsum('tk,tjkc->jc', factor, window)
        return lax.fori_loop(0, SPAN, add_offset, jnp.zeros((NLON, C), jnp.float32))
    return lax.map(one_row, jnp.arange(NLAT, dtype=jnp.int32))

def channel_mix(stacked, weight):
    flat = jnp.dot(stacked.reshape(-1, K * C), weight.reshape(K * C, C), preferred_element_type=jnp.float32)
    return flat.reshape(NLAT, NLON, C)

def back_mix(grad_out, weight):
    flat = jnp.dot(grad_out.reshape(-1, C), weight.reshape(K * C, C).T, preferred_element_type=jnp.float32)
    return flat.astype(jnp.bfloat16).reshape(NLAT, NLON, K, C)

def weight_grad(stacked, grad_out):
    summed = lax.dot_general(stacked.reshape(-1, K * C), grad_out.reshape(-1, C), (((0,), (0,)), ((), ())), preferred_element_type=jnp.float32)
    return (summed * (1.0 / math.sqrt(NLAT * NLON))).reshape(K, C, C)

def reference(features, cotangent, basis, support, weight_one, weight_two):
    filtered = mask_filter(basis, support)
    y_one = stencil(features, filtered)
    z_one = channel_mix(y_one, weight_one)
    hidden = jax.nn.silu(z_one).astype(jnp.bfloat16)
    y_two = stencil(hidden, filtered)
    layer_out = channel_mix(y_two, weight_two).astype(jnp.bfloat16)
    dy_two = back_mix(cotangent, weight_two)
    grad_two = weight_grad(y_two, cotangent)
    sigma = jax.nn.sigmoid(z_one)
    dz_one = (transposed(dy_two, filtered) * sigma * (1.0 + z_one * (1.0 - sigma))).astype(jnp.bfloat16)
    dy_one = back_mix(dz_one, weight_one)
    grad_one = weight_grad(y_one, dz_one)
    grad_input = transposed(dy_one, filtered).astype(jnp.bfloat16)
    return (layer_out, grad_input, grad_one, grad_two)
```

```python
import functools
import math

import jax
import jax.numpy as jnp
from jax import lax
from jax.experimental import pallas as pl
from jax.experimental.pallas import tpu as pltpu
from jax.sharding import PartitionSpec as P

HW = 16
WIDE = 128
MESH = pl.DeviceIdType.MESH
BF = jnp.bfloat16
F32 = jnp.float32
NT = (((1,), (1,)), ((), ()))
TN = (((0,), (0,)), ((), ()))


def dot(a, b, dims=(((1,), (0,)), ((), ()))):
    return lax.dot_general(a, b, dims, preferred_element_type=F32)


def kernel(
    dims,
    f_ref,
    c_ref,
    tf_ref,
    tb_ref,
    w1_ref,
    w2_ref,
    out_ref,
    gin_ref,
    g1_ref,
    g2_ref,
    ext_f,
    ext_c,
    ext_h,
    ext_d,
    tails,
    taps,
    band,
    back,
    y1,
    y2,
    dsig,
    dy,
    part,
    p32,
    gb,
    r1,
    sb,
    r2,
    s3,
    r3,
    r4,
    rowtmp,
    gfull,
    halo_snd,
    halo_rcv,
    tap_snd,
    tap_rcv,
    core_snd,
    core_rcv,
    x_snd,
    x_rcv,
    yz_snd,
    yz_rcv,
):
    nx, nyl, nz, nyh, rows, cols, chans, basis, scaling = dims
    own = -(-cols // 16) * 16
    right = own
    left = WIDE - HW
    nlat, nlon = nx * nyl * 2, nz * nyh
    ny = nyl * nyh
    nyz = nz * ny
    blk = 4
    nblk = rows // blk

    lat = lax.axis_index("lat")
    lon = lax.axis_index("lon")
    my_x = lat // (nyl * 2)
    my_core = lat % 2
    my_y = (lon % nyh) * nyl + (lat // 2) % nyl
    my_z = lon // nyh
    me_yz = my_z * ny + my_y
    north, south = (lat + nlat - 1) % nlat, (lat + 1) % nlat
    west, east = (lon + nlon - 1) % nlon, (lon + 1) % nlon

    def yz_device(idx):
        z, y = idx // ny, idx % ny
        return my_x * (nyl * 2) + (y % nyl) * 2 + my_core, z * nyh + y // nyl

    def x_device(x):
        return x * (nyl * 2) + lat % (nyl * 2), lon

    partner = (lat + 1 - 2 * my_core, lon)
    around = [
        (lat, east),
        (lat, west),
        (south, lon),
        (north, lon),
        (south, east),
        (north, east),
        (south, west),
        (north, west),
    ]

    barrier = pltpu.get_barrier_semaphore()

    def greet(device):
        pl.semaphore_signal(barrier, inc=1, device_id=device, device_id_type=MESH)

    for device in around:
        greet(device)
    greet(partner)
    for d in range(1, nx):
        greet(x_device((my_x + d) % nx))

    def greet_yz(d, carry):
        greet(yz_device((me_yz + d) % nyz))
        return carry

    lax.fori_loop(1, nyz, greet_yz, 0)

    def put_tail(field, r, value):
        tails[field, r] = value[cols - HW : cols].astype(BF)

    def stage(field, src, ext):
        def body(r, carry):
            value = src[r].astype(F32)
            wide = jnp.concatenate([value, jnp.zeros((own - cols, chans), F32)], axis=0)
            ext[r + 1, pl.ds(0, own)] = wide.astype(BF)
            put_tail(field, r, value)
            return carry

        lax.fori_loop(0, rows, body, 0)

    def halo(field, ext):
        tail = tails.at[field]
        body = pl.ds(1, rows)
        moves = [
            (tail, ext.at[body, pl.ds(left, HW)]),
            (ext.at[body, pl.ds(0, HW)], ext.at[body, pl.ds(right, HW)]),
            (ext.at[rows, pl.ds(0, own)], ext.at[0, pl.ds(0, own)]),
            (ext.at[1, pl.ds(0, own)], ext.at[rows + 1, pl.ds(0, own)]),
            (tail.at[rows - 1], ext.at[0, pl.ds(left, HW)]),
            (tail.at[0], ext.at[rows + 1, pl.ds(left, HW)]),
            (ext.at[rows, pl.ds(0, HW)], ext.at[0, pl.ds(right, HW)]),
            (ext.at[1, pl.ds(0, HW)], ext.at[rows + 1, pl.ds(right, HW)]),
        ]
        return [
            pltpu.make_async_remote_copy(
                src_ref=src,
                dst_ref=dst,
                send_sem=halo_snd.at[field, i],
                recv_sem=halo_rcv.at[field, i],
                device_id=around[i],
                device_id_type=MESH,
            )
            for i, (src, dst) in enumerate(moves)
        ]

    def tap_copies():
        return [
            pltpu.make_async_remote_copy(
                src_ref=taps.at[src],
                dst_ref=taps.at[dst],
                send_sem=tap_snd.at[i],
                recv_sem=tap_rcv.at[i],
                device_id=device,
                device_id_type=MESH,
            )
            for i, (src, dst, device) in enumerate(
                [(rows, 0, (south, lon)), (1, rows + 1, (north, lon))]
            )
        ]

    def start(copies):
        for copy in copies:
            copy.start()

    def arrive(copies):
        for copy in copies:
            copy.wait_recv()

    stage(0, f_ref, ext_f)
    stage(1, c_ref, ext_c)
    taps[pl.ds(1, rows)] = tb_ref[...]
    pl.semaphore_wait(barrier, len(around) + 1 + (nx - 1) + (nyz - 1))
    start(halo(0, ext_f))
    start(tap_copies())
    start(halo(1, ext_c))

    low = own - 24
    lane = lax.broadcasted_iota(jnp.int32, (24, WIDE), 1)
    cell = lax.broadcasted_iota(jnp.int32, (24, WIDE), 0) + low
    valid = cell < cols
    plain = valid & ((lane < cols) | (lane >= left))
    moved = valid & (lane >= right) & (lane < left)
    gap = own - cols

    def toeplitz(tap):
        wide = jnp.broadcast_to(tap, (own, WIDE))
        t = pltpu.roll(wide, 0, 1, stride=1, stride_axis=0)
        t6 = pltpu.roll(wide[:24], low + gap, 1, stride=1, stride_axis=0)
        bottom = jnp.where(moved, t6, jnp.where(plain, t[low:], 0.0))
        return jnp.concatenate([t[:low], bottom], axis=0).astype(BF)

    def build_fwd(r, carry):
        for k in range(basis):
            for a in range(3):
                tap = tf_ref[r, pl.ds(k * 3 + a, 1), :]
                band[r, pl.ds(k * own, own), pl.ds(a * WIDE, WIDE)] = toeplitz(tap)
        return carry

    lax.fori_loop(0, rows, build_fwd, 0)

    def build_back(i, sides=(0, 1, 2), keep=None):
        for k in range(basis):
            for a in sides:
                tap = taps[i, pl.ds(k * 3 + a, 1), :]
                if keep is not None:
                    tap = jnp.where(keep, tap, 0.0)
                back[i, pl.ds(a * own, own), pl.ds(k * WIDE, WIDE)] = toeplitz(tap)

    def build_back_loop(i, carry):
        build_back(i)
        return carry

    lax.fori_loop(1, rows + 1, build_back_loop, 0)

    def stencil(ext, y, r):
        x = ext[pl.ds(r, 3)].reshape(3 * WIDE, chans)
        t = dot(band[r], x).astype(BF)
        for k in range(basis):
            y[r, :, pl.ds(k * chans, chans)] = t[k * own : (k + 1) * own]

    def mix(y, w_ref, r0):
        flat = y[pl.ds(r0, blk)].reshape(blk * own, basis * chans)
        return dot(flat, w_ref[...].reshape(basis * chans, chans))

    arrive(halo(0, ext_f))

    def first(b, carry):
        r0 = b * blk
        for i in range(blk):
            stencil(ext_f, y1, r0 + i)
        z = mix(y1, w1_ref, r0)
        sigma = jax.nn.sigmoid(z)
        dsig[pl.ds(r0, blk)] = (sigma * (1.0 + z * (1.0 - sigma))).reshape(blk, own, chans)
        hidden = (z * sigma).reshape(blk, own, chans)
        ext_h[pl.ds(r0 + 1, blk), pl.ds(0, own)] = hidden.astype(BF)
        for i in range(blk):
            put_tail(2, r0 + i, hidden[i])
        return carry

    lax.fori_loop(0, nblk, first, 0)
    start(halo(2, ext_h))

    def spread_rows(ext, w_ref, i0, count):
        flat = ext[pl.ds(i0, count)].reshape(count * WIDE, chans)
        for k in range(basis):
            d = dot(flat, w_ref[k], NT).astype(BF)
            dy[pl.ds(i0, count), k] = d.reshape(count, WIDE, chans)

    def spread(ext, w_ref):
        def body(b, carry):
            i0 = 1 + b * blk
            spread_rows(ext, w_ref, i0, blk)
            for i in range(blk):
                u = dy[i0 + i].reshape(basis * WIDE, chans)
                part[i0 + i] = dot(back[i0 + i], u).reshape(3, own, chans)
            return carry

        lax.fori_loop(0, nblk, body, 0)
        for i, a in ((0, 2), (rows + 1, 0)):
            spread_rows(ext, w_ref, i, 1)
            u = dy[i].reshape(basis * WIDE, chans)
            part[i, a] = dot(back[i, pl.ds(a * own, own)], u)

    def gathered(r0):
        return (
            part[pl.ds(r0, blk), 2] + part[pl.ds(r0 + 1, blk), 1] + part[pl.ds(r0 + 2, blk), 0]
        )

    arrive(tap_copies())
    build_back(0, (2,), lat > 0)
    build_back(rows + 1, (0,), lat < nlat - 1)
    arrive(halo(1, ext_c))
    spread(ext_c, w2_ref)

    def activation(b, carry):
        r0 = b * blk
        dz = gathered(r0) * dsig[pl.ds(r0, blk)]
        ext_d[pl.ds(r0 + 1, blk), pl.ds(0, own)] = dz.astype(BF)
        for i in range(blk):
            put_tail(3, r0 + i, dz[i])
        return carry

    lax.fori_loop(0, nblk, activation, 0)
    start(halo(3, ext_d))

    chunk = basis * chans // (2 * nx)
    piece = chunk // nyz

    def weight_grad(g, y, ext):
        flat = y[...].reshape(rows * own, basis * chans)
        grad = ext[pl.ds(1, rows), pl.ds(0, own)].reshape(rows * own, chans)
        p32[g] = dot(flat, grad, TN).reshape(2, nx, chunk, chans)
        gb[g] = p32[g, 1 - my_core].astype(BF)

    def remote(src, dst, snd, rcv, device):
        return pltpu.make_async_remote_copy(
            src_ref=src,
            dst_ref=dst,
            send_sem=snd,
            recv_sem=rcv,
            device_id=device,
            device_id_type=MESH,
        )

    def core_scatter(g):
        return [remote(gb.at[g], r1.at[g], core_snd.at[g, 0], core_rcv.at[g, 0], partner)]

    def x_scatter(g):
        return [
            remote(
                sb.at[g, (my_x + d) % nx],
                r2.at[g, d - 1],
                x_snd.at[g, 0, d],
                x_rcv.at[g, 0, d],
                x_device((my_x + d) % nx),
            )
            for d in range(1, nx)
        ]

    def yz_scatter(g, d):
        peer = (me_yz + d) % nyz
        return remote(
            s3.at[g, peer],
            r3.at[g, me_yz],
            yz_snd.at[g, 0, d],
            yz_rcv.at[g, 0, d],
            yz_device(peer),
        )

    def yz_gather(g, d):
        peer = (me_yz + d) % nyz
        return remote(
            r4.at[g, me_yz],
            r4.at[g, me_yz],
            yz_snd.at[g, 1, d],
            yz_rcv.at[g, 1, d],
            yz_device(peer),
        )

    def x_gather(g):
        return [
            remote(
                gfull.at[g, my_core, my_x],
                gfull.at[g, my_core, my_x],
                x_snd.at[g, 1, d],
                x_rcv.at[g, 1, d],
                x_device((my_x + d) % nx),
            )
            for d in range(1, nx)
        ]

    def core_gather(g):
        return [
            remote(
                gfull.at[g, my_core],
                gfull.at[g, my_core],
                core_snd.at[g, 1],
                core_rcv.at[g, 1],
                partner,
            )
        ]

    def start_yz(make, g):
        def body(d, carry):
            make(g, d).start()
            return carry

        lax.fori_loop(1, nyz, body, 0)

    def arrive_yz(make, g):
        def body(d, carry):
            make(g, d).wait_recv()
            return carry

        lax.fori_loop(1, nyz, body, 0)

    def sent_yz(make, g):
        def body(d, carry):
            make(g, d).wait_send()
            return carry

        lax.fori_loop(1, nyz, body, 0)

    def reduce_core(g):
        arrive(core_scatter(g))
        sb[g] = (p32[g, my_core] + r1[g].astype(F32)).astype(BF)
        start(x_scatter(g))

    def reduce_x(g):
        arrive(x_scatter(g))
        total = p32[g, my_core, my_x] + r1[g, my_x].astype(F32)
        for d in range(1, nx):
            total = total + r2[g, d - 1].astype(F32)
        for i in range(nyz):
            s3[g, i] = total[i * piece : (i + 1) * piece]
        start_yz(yz_scatter, g)

    def reduce_yz(g):
        r3[g, me_yz] = s3[g, me_yz]
        arrive_yz(yz_scatter, g)
        total = r3[g, 0]
        for i in range(1, nyz):
            total = total + r3[g, i]
        r4[g, me_yz] = total * scaling
        start_yz(yz_gather, g)

    def gather_yz(g):
        arrive_yz(yz_gather, g)
        for i in range(nyz):
            rowtmp[g, pl.ds(i * piece, piece)] = r4[g, i]
        gfull[g, my_core, my_x] = rowtmp[g].astype(BF)
        start(x_gather(g))

    def gather_x(g):
        arrive(x_gather(g))
        start(core_gather(g))

    def gather_core(g, ref):
        arrive(core_gather(g))
        ref[...] = gfull[g].astype(F32).reshape(basis * chans, chans)

    weight_grad(0, y1, ext_d)
    start(core_scatter(0))

    arrive(halo(2, ext_h))

    def second(b, carry):
        for i in range(blk):
            stencil(ext_h, y2, b * blk + i)
        return carry

    lax.fori_loop(0, nblk, second, 0)
    weight_grad(1, y2, ext_c)
    start(core_scatter(1))
    reduce_core(0)

    def second_mix(b, carry):
        r0 = b * blk
        z = mix(y2, w2_ref, r0).reshape(blk, own, chans)
        out_ref[pl.ds(r0, blk)] = z[:, :cols].astype(BF)
        return carry

    lax.fori_loop(0, nblk, second_mix, 0)
    reduce_x(0)
    reduce_core(1)

    arrive(halo(3, ext_d))
    spread(ext_d, w1_ref)
    reduce_yz(0)
    reduce_x(1)

    def finish(b, carry):
        r0 = b * blk
        gin_ref[pl.ds(r0, blk)] = gathered(r0)[:, :cols].astype(BF)
        return carry

    lax.fori_loop(0, nblk, finish, 0)
    reduce_yz(1)
    gather_yz(0)
    gather_yz(1)
    gather_x(0)
    gather_x(1)
    gather_core(0, g1_ref)
    gather_core(1, g2_ref)

    for field, ext in enumerate((ext_f, ext_c, ext_h, ext_d)):
        for copy in halo(field, ext):
            copy.wait_send()
    for copy in tap_copies():
        copy.wait_send()
    for g in range(2):
        for copy in core_scatter(g) + x_scatter(g) + x_gather(g) + core_gather(g):
            copy.wait_send()
        sent_yz(yz_scatter, g)
        sent_yz(yz_gather, g)


def tap_rows(taps):
    reach = taps.ndim * ((0, 0),)
    half = jnp.pad(taps, reach[:-1] + ((0, WIDE - 2 * HW - 1),))
    return jnp.roll(half, -HW, axis=-1).reshape(taps.shape[0], -1, WIDE)


def local(sizes, features, cotangent, basis, support, weight_one, weight_two):
    nx, nyl, nz, nyh = sizes
    rows, cols, chans = features.shape
    count = weight_one.shape[0]
    nlat, nlon = nx * nyl * 2, nz * nyh
    nyz = nyl * nyh * nz
    scaling = 1.0 / math.sqrt(rows * nlat * cols * nlon)
    own = -(-cols // 16) * 16
    chunk = count * chans // (2 * nx)
    piece = chunk // nyz

    lat = lax.axis_index("lat")
    offset = jnp.abs(jnp.arange(2 * HW + 1, dtype=jnp.int32) - HW)
    inside = offset[None, :] <= support[:, None]
    filtered = jnp.where(inside[:, None, None, :], basis, jnp.zeros_like(basis)).astype(F32)
    row = lax.broadcasted_iota(jnp.int32, (rows, 1, 3, 1), 0) + lat * rows
    side = lax.broadcasted_iota(jnp.int32, (rows, 1, 3, 1), 2) - 1
    exists = (row + side >= 0) & (row + side < rows * nlat)
    fwd_taps = tap_rows(jnp.where(exists, filtered, 0.0))
    back_taps = tap_rows(filtered[..., ::-1])

    vmem = pl.BlockSpec(memory_space=pltpu.VMEM)
    dma = pltpu.SemaphoreType.DMA
    ext = pltpu.VMEM((rows + 2, WIDE, chans), BF)
    out = pl.pallas_call(
        functools.partial(
            kernel, (nx, nyl, nz, nyh, rows, cols, chans, count, scaling)
        ),
        out_shape=(
            jax.ShapeDtypeStruct(features.shape, BF),
            jax.ShapeDtypeStruct(features.shape, BF),
            jax.ShapeDtypeStruct((count * chans, chans), F32),
            jax.ShapeDtypeStruct((count * chans, chans), F32),
        ),
        in_specs=[vmem] * 6,
        out_specs=(vmem,) * 4,
        scratch_shapes=[
            ext,
            ext,
            ext,
            ext,
            pltpu.VMEM((4, rows, HW, chans), BF),
            pltpu.VMEM((rows + 2, count * 3, WIDE), F32),
            pltpu.VMEM((rows, count * own, 3 * WIDE), BF),
            pltpu.VMEM((rows + 2, 3 * own, count * WIDE), BF),
            pltpu.VMEM((rows, own, count * chans), BF),
            pltpu.VMEM((rows, own, count * chans), BF),
            pltpu.VMEM((rows, own, chans), F32),
            pltpu.VMEM((rows + 2, count, WIDE, chans), BF),
            pltpu.VMEM((rows + 2, 3, own, chans), F32),
            pltpu.VMEM((2, 2, nx, chunk, chans), F32),
            pltpu.VMEM((2, nx, chunk, chans), BF),
            pltpu.VMEM((2, nx, chunk, chans), BF),
            pltpu.VMEM((2, nx, chunk, chans), BF),
            pltpu.VMEM((2, nx - 1, chunk, chans), BF),
            pltpu.VMEM((2, nyz, piece, chans), F32),
            pltpu.VMEM((2, nyz, piece, chans), F32),
            pltpu.VMEM((2, nyz, piece, chans), F32),
            pltpu.VMEM((2, chunk, chans), F32),
            pltpu.VMEM((2, 2, nx, chunk, chans), BF),
            dma((4, 8)),
            dma((4, 8)),
            dma((2,)),
            dma((2,)),
            dma((2, 2)),
            dma((2, 2)),
            dma((2, 2, nx)),
            dma((2, 2, nx)),
            dma((2, 2, nyz)),
            dma((2, 2, nyz)),
        ],
        compiler_params=pltpu.CompilerParams(
            collective_id=0, has_side_effects=True, vmem_limit_bytes=60 * 1024 * 1024
        ),
    )(features, cotangent, fwd_taps, back_taps, weight_one, weight_two)
    shape = weight_one.shape
    return out[0], out[1], out[2].reshape(shape), out[3].reshape(shape)


def solution(mesh):
    nlat, nlon = mesh.shape["lat"], mesh.shape["lon"]
    nyl = 2 if nlat >= 16 else 1
    sizes = (nlat // (2 * nyl), nyl, nlon // 2, 2)
    placed = (
        P("lat", "lon", None),
        P("lat", "lon", None),
        P("lat", None, None, None),
        P("lat"),
        P(),
        P(),
    )
    return jax.shard_map(
        functools.partial(local, sizes),
        mesh=mesh,
        in_specs=placed,
        out_specs=(P("lat", "lon", None), P("lat", "lon", None), P(), P()),
        check_vma=False,
    )
```

```python
import functools
import math

import jax
import jax.numpy as jnp
from jax import lax
from jax.experimental import pallas as pl
from jax.experimental.pallas import tpu as pltpu
from jax.sharding import PartitionSpec as P

HW = 16
SPAN = 2 * HW + 1
WIDE = 128
MESH = pl.DeviceIdType.MESH
BF = jnp.bfloat16
F32 = jnp.float32
NN = (((1,), (0,)), ((), ()))
NT = (((1,), (1,)), ((), ()))
TN = (((0,), (0,)), ((), ()))


def dot(a, b, dims=NN):
    return lax.dot_general(a, b, dims, preferred_element_type=F32)


def iota(shape, dim):
    return lax.broadcasted_iota(jnp.int32, shape, dim)


def kernel(
    dims,
    f_ref,
    c_ref,
    basis_ref,
    support_ref,
    w1_ref,
    w2_ref,
    out_ref,
    gin_ref,
    grad_ref,
    raw_f,
    raw_c,
    w1,
    w2,
    w1t,
    w2t,
    perm,
    ext_f,
    ext_c,
    ext_h,
    ext_d,
    tails,
    loose,
    taps,
    edge_out,
    edge_in,
    band,
    back,
    y1,
    v2,
    tmp,
    dsig,
    natural,
    turned,
    p32,
    gb,
    r1,
    sb,
    r2,
    ty,
    sy,
    ry,
    s3,
    r3,
    r4,
    rowtmp,
    gfull,
    in_sem,
    out_sem,
    halo_snd,
    halo_rcv,
    tap_snd,
    tap_rcv,
    core_snd,
    core_rcv,
    x_snd,
    x_rcv,
    y_snd,
    y_rcv,
    z_snd,
    z_rcv,
):
    nx, nyl, nz, nyh, rows, cols, chans, basis, scaling = dims
    own = -(-cols // 16) * 16
    right = own
    left = WIDE - HW
    nlat, nlon = nx * nyl * 2, nz * nyh
    ny = nyl * nyh
    blk = 4
    nblk = rows // blk
    wide_chans = basis * chans

    inputs = [
        pltpu.make_async_copy(src, dst, in_sem.at[i])
        for i, (src, dst) in enumerate(
            [
                (f_ref, raw_f.at[pl.ds(0, cols)]),
                (c_ref, raw_c.at[pl.ds(0, cols)]),
                (w1_ref, w1),
                (w2_ref, w2),
            ]
        )
    ]
    for copy in inputs:
        copy.start()

    lat = lax.axis_index("lat")
    lon = lax.axis_index("lon")

    def wrap(value, count):
        return jnp.where(value >= count, value - count, value)

    my_x = lat // (nyl * 2)
    in_x = lat - my_x * (nyl * 2)
    my_yl = in_x // 2
    my_core = in_x - my_yl * 2
    my_z = lon // nyh
    my_y = (lon - my_z * nyh) * nyl + my_yl
    north, south = wrap(lat + nlat - 1, nlat), wrap(lat + 1, nlat)
    west, east = wrap(lon + nlon - 1, nlon), wrap(lon + 1, nlon)

    partner = (lat + 1 - 2 * my_core, lon)
    around = [
        (lat, east),
        (lat, west),
        (south, lon),
        (north, lon),
        (south, east),
        (north, east),
        (south, west),
        (north, west),
    ]
    x_peers = [wrap(my_x + d, nx) for d in range(nx)]
    x_devices = [(x * (nyl * 2) + in_x, lon) for x in x_peers]
    x_from = [wrap(my_x + nx - d, nx) for d in range(nx)]
    y_peers = [wrap(my_y + d, ny) for d in range(ny)]
    z_peers = [wrap(my_z + d, nz) for d in range(nz)]
    my_yh = lon - my_z * nyh
    y_devices = []
    for y in y_peers:
        yh = y // nyl
        y_devices.append((my_x * (nyl * 2) + (y - yh * nyl) * 2 + my_core, my_z * nyh + yh))
    z_devices = [(lat, z * nyh + my_yh) for z in z_peers]

    barrier = pltpu.get_barrier_semaphore()

    def greet(device):
        pl.semaphore_signal(barrier, inc=1, device_id=device, device_id_type=MESH)

    for device in around:
        greet(device)
    others = z_devices[1:] + x_devices[1:] + y_devices[1:] + [partner]
    for device in others:
        greet(device)

    side = HW * HW
    i0, i1 = iota((side, side), 0), iota((side, side), 1)
    perm[...] = jnp.where(i1 == (i0 & 15) * HW + (i0 >> 4), 1.0, 0.0).astype(BF)

    def turn(block):
        return dot(perm[...], block.reshape(side, chans)).astype(BF).reshape(HW, HW, chans)

    def stage(field, raw, ext):
        raw[pl.ds(cols, own - cols)] = jnp.zeros((own - cols, rows, chans), BF)
        tails[field] = turn(raw[pl.ds(cols - HW, HW)])
        for b in range(own // HW):
            ext[pl.ds(1, rows), pl.ds(b * HW, HW)] = turn(raw[pl.ds(b * HW, HW)])

    def remote(src, dst, snd, rcv, device):
        return pltpu.make_async_remote_copy(
            src_ref=src,
            dst_ref=dst,
            send_sem=snd,
            recv_sem=rcv,
            device_id=device,
            device_id_type=MESH,
        )

    def halo(field, ext, parts=(0, 1)):
        tail = tails.at[field]
        top = rows // 2 + 1
        upper, lower = pl.ds(1, top), pl.ds(1 + top, rows - top)
        moves = [
            [
                (tail.at[pl.ds(0, top)], ext.at[upper, pl.ds(left, HW)], 0),
                (ext.at[upper, pl.ds(0, HW)], ext.at[upper, pl.ds(right, HW)], 1),
                (ext.at[rows, pl.ds(0, own)], ext.at[0, pl.ds(0, own)], 2),
                (tail.at[rows - 1], ext.at[0, pl.ds(left, HW)], 4),
                (ext.at[rows, pl.ds(0, HW)], ext.at[0, pl.ds(right, HW)], 6),
            ],
            [
                (tail.at[pl.ds(top, rows - top)], ext.at[lower, pl.ds(left, HW)], 0),
                (ext.at[lower, pl.ds(0, HW)], ext.at[lower, pl.ds(right, HW)], 1),
                (ext.at[1, pl.ds(0, own)], ext.at[rows + 1, pl.ds(0, own)], 3),
                (tail.at[0], ext.at[rows + 1, pl.ds(left, HW)], 5),
                (ext.at[1, pl.ds(0, HW)], ext.at[rows + 1, pl.ds(right, HW)], 7),
            ],
        ]
        return [
            remote(src, dst, halo_snd.at[field, part, i], halo_rcv.at[field, part, i], around[to])
            for part in parts
            for i, (src, dst, to) in enumerate(moves[part])
        ]

    def tap_copies():
        return [
            remote(edge_out.at[i], edge_in.at[i], tap_snd.at[i], tap_rcv.at[i], device)
            for i, device in enumerate([(south, lon), (north, lon)])
        ]

    def start(copies):
        for copy in copies:
            copy.start()

    def arrive(copies):
        for copy in copies:
            copy.wait_recv()

    def sent(copies):
        for copy in copies:
            copy.wait_send()

    inputs[0].wait()
    stage(0, raw_f, ext_f)
    pl.semaphore_wait(barrier, len(around) + len(others))
    start(halo(0, ext_f))

    loose[...] = jnp.zeros(loose.shape, F32)
    row = iota((rows, WIDE), 0)
    lane = iota((rows, WIDE), 1)
    reach = jnp.zeros((rows, WIDE), jnp.int32)
    for r in range(rows):
        reach = jnp.where(row == r, support_ref[r], reach)
    inside = jnp.abs(lane - HW) <= reach
    for k in range(basis):
        for a in range(3):
            loose[k * 3 + a, :, pl.ds(0, SPAN)] = basis_ref[k, a].astype(F32)
    b0, b1 = iota((WIDE, 2 * WIDE), 0), iota((WIDE, 2 * WIDE), 1)
    place = (b1 == ((b0 - HW) & (WIDE - 1))) | (b1 == ((HW - b0) & (WIDE - 1)) + WIDE)
    place = jnp.where(place, 1.0, 0.0).astype(BF)
    for k in range(basis):
        for a in range(3):
            ka = k * 3 + a
            masked = jnp.where(inside, loose[ka], 0.0).astype(BF)
            placed = dot(masked, place)
            edge_out[0, pl.ds(ka, 1)] = placed[rows - 1 : rows, WIDE:]
            edge_out[1, pl.ds(ka, 1)] = placed[:1, WIDE:]
            forward = placed[:, :WIDE]
            if a == 0:
                forward = jnp.where((row == 0) & (lat == 0), 0.0, forward)
            elif a == 2:
                forward = jnp.where((row == rows - 1) & (lat == nlat - 1), 0.0, forward)
            for r in range(rows):
                taps[r, pl.ds(ka, 1), pl.ds(0, WIDE)] = forward[r : r + 1]
                taps[r, pl.ds(ka, 1), pl.ds(WIDE, WIDE)] = placed[r : r + 1, WIDE:]
    start(tap_copies())

    low = own - 24
    lane24 = iota((24, WIDE), 1)
    valid = iota((24, WIDE), 0) + low < cols
    plain = valid & ((lane24 < cols) | (lane24 >= left))
    moved = valid & (lane24 >= right) & (lane24 < left)
    gap = own - cols

    def toeplitz(tap):
        wide = jnp.broadcast_to(tap, (own, WIDE))
        t = pltpu.roll(wide, 0, 1, stride=1, stride_axis=0)
        t6 = pltpu.roll(wide[:24], low + gap, 1, stride=1, stride_axis=0)
        bottom = jnp.where(moved, t6, jnp.where(plain, t[low:], 0.0))
        return jnp.concatenate([t[:low], bottom], axis=0).astype(BF)

    def build_fwd(r, carry):
        for k in range(basis):
            for a in range(3):
                tap = taps[r, pl.ds(k * 3 + a, 1), pl.ds(0, WIDE)]
                band[r, pl.ds(k * own, own), pl.ds(a * WIDE, WIDE)] = toeplitz(tap)
        return carry

    def build_back(r, carry):
        for k in range(basis):
            for a in range(3):
                tap = taps[r, pl.ds(k * 3 + a, 1), pl.ds(WIDE, WIDE)]
                t = 2 - a
                back[r + a, pl.ds(k * own, own), pl.ds(t * WIDE, WIDE)] = toeplitz(tap)
        return carry

    lax.fori_loop(0, rows, build_fwd, 0)

    inputs[1].wait()
    stage(1, raw_c, ext_c)
    inputs[2].wait()
    inputs[3].wait()
    eye = jnp.where(iota((chans, chans), 0) == iota((chans, chans), 1), 1.0, 0.0).astype(BF)
    for k in range(basis):
        w1t[k] = dot(eye, w1[k], NT).astype(BF)
        w2t[k] = dot(eye, w2[k], NT).astype(BF)
    lax.fori_loop(0, rows, build_back, 0)

    def stencil(ext, matrix, at, y, r):
        x = ext[pl.ds(r, 3)].reshape(3 * WIDE, chans)
        t = dot(matrix[r + at], x).astype(BF)
        for k in range(basis):
            y[r, :, pl.ds(k * chans, chans)] = t[k * own : (k + 1) * own]

    def convolve(ext, matrix, at, y, w, r0):
        for i in range(blk):
            stencil(ext, matrix, at, y, r0 + i)
        flat = y[pl.ds(r0, blk)].reshape(blk * own, wide_chans)
        return dot(flat, w[...].reshape(wide_chans, chans))

    def put(field, ext, r0, value):
        value = value.reshape(blk, own, chans)
        ext[pl.ds(r0 + 1, blk), pl.ds(0, own)] = value.astype(BF)
        for i in range(blk):
            tails[field, r0 + i] = value[i, cols - HW : cols].astype(BF)

    def first(b, carry):
        r0 = b * blk
        z = convolve(ext_f, band, 0, y1, w1, r0)
        sigma = jax.nn.sigmoid(z)
        dsig[pl.ds(r0, blk)] = (sigma * (1.0 + z * (1.0 - sigma))).reshape(blk, own, chans)
        put(2, ext_h, r0, z * sigma)
        return carry

    def first_back(b, carry):
        r0 = b * blk
        g = convolve(ext_c, back, 1, v2, w2t, r0)
        put(3, ext_d, r0, g * dsig[pl.ds(r0, blk)].reshape(blk * own, chans))
        return carry

    def second(b, carry):
        r0 = b * blk
        z = convolve(ext_h, band, 0, tmp, w2, r0)
        natural[0, pl.ds(r0, blk)] = z.astype(BF).reshape(blk, own, chans)
        return carry

    def second_back(b, carry):
        r0 = b * blk
        z = convolve(ext_d, back, 1, tmp, w1t, r0)
        natural[1, pl.ds(r0, blk)] = z.astype(BF).reshape(blk, own, chans)
        return carry

    def outgoing(i, ref):
        return pltpu.make_async_copy(turned.at[i, pl.ds(0, cols)], ref, out_sem.at[i])

    def emit(i, ref):
        for b in range(own // HW):
            turned[i, pl.ds(b * HW, HW)] = turn(natural[i, :, pl.ds(b * HW, HW)])
        outgoing(i, ref).start()

    chunk = wide_chans // nx
    half = chunk // 2
    slab = chunk // ny
    piece = slab // nz
    far_first = sorted(range(1, nx), key=lambda d: -min(d, nx - d))
    near_first = far_first[::-1]

    def core_scatter(d):
        x = x_peers[d]
        return remote(gb.at[x], r1.at[x], core_snd.at[0, d], core_rcv.at[0, d], partner)

    def x_scatter(d):
        src, dst = sb.at[x_peers[d]], r2.at[d - 1]
        return remote(src, dst, x_snd.at[0, d], x_rcv.at[0, d], x_devices[d])

    def y_scatter(d):
        src, dst = sy.at[y_peers[d]], ry.at[d - 1]
        return remote(src, dst, y_snd.at[0, d], y_rcv.at[0, d], y_devices[d])

    def z_scatter(d):
        src, dst = s3.at[z_peers[d]], r3.at[d - 1]
        return remote(src, dst, z_snd.at[0, d], z_rcv.at[0, d], z_devices[d])

    def z_gather(d):
        mine = r4.at[my_z]
        return remote(mine, mine, z_snd.at[1, d], z_rcv.at[1, d], z_devices[d])

    def y_gather(d):
        mine = gfull.at[my_core, my_x, my_y]
        return remote(mine, mine, y_snd.at[1, d], y_rcv.at[1, d], y_devices[d])

    def x_gather(d):
        mine = gfull.at[my_core, my_x]
        return remote(mine, mine, x_snd.at[1, d], x_rcv.at[1, d], x_devices[d])

    def core_gather(d):
        mine = gfull.at[my_core, x_from[d]]
        return remote(mine, mine, core_snd.at[1, d], core_rcv.at[1, d], partner)

    def every(make, count):
        return [make(d) for d in range(1, count)]

    def keep_grad(g, value, first):
        for core in range(2):
            for x in range(nx):
                at = (core * nx + x) * half
                to = (core, x, pl.ds(g * half, half))
                share = value[at : at + half]
                p32[to] = share if first else p32[to] + share

    def reduce_core():
        for d in far_first:
            x = x_peers[d]
            core_scatter(d).wait_recv()
            sb[x] = (p32[my_core, x] + r1[x].astype(F32)).astype(BF)
            x_scatter(d).start()
        core_scatter(0).wait_recv()

    def reduce_x():
        arrive(every(x_scatter, nx))
        total = p32[my_core, my_x] + r1[my_x].astype(F32)
        for d in range(1, nx):
            total = total + r2[d - 1].astype(F32)
        ty[...] = total.reshape(ny, slab, chans)
        sy[...] = total.astype(BF).reshape(ny, slab, chans)
        start(every(y_scatter, ny))

    def reduce_y():
        arrive(every(y_scatter, ny))
        total = ty[my_y]
        for d in range(1, ny):
            total = total + ry[d - 1].astype(F32)
        for i in range(nz):
            s3[i] = total[i * piece : (i + 1) * piece]
        start(every(z_scatter, nz))

    def reduce_z():
        arrive(every(z_scatter, nz))
        r4[my_z] = (s3[my_z] + jnp.sum(r3[...], axis=0)) * scaling
        start(every(z_gather, nz))

    def gather_z():
        arrive(every(z_gather, nz))
        for i in range(nz):
            rowtmp[pl.ds(i * piece, piece)] = r4[i]
        gfull[my_core, my_x, my_y] = rowtmp[...].astype(BF)
        start(every(y_gather, ny))

    def gather_y():
        arrive(every(y_gather, ny))
        start([x_gather(d) for d in far_first])
        core_gather(0).start()

    def gather_x():
        for d in near_first:
            x_gather(d).wait_recv()
            core_gather(d).start()
        for d in range(nx):
            core_gather(d).wait_recv()

    def mine(ext, r0, count):
        return ext[pl.ds(r0 + 1, count), pl.ds(0, own)].reshape(count * own, chans)

    def weight_grads(r0, count, first):
        flat = v2[pl.ds(r0, count)].reshape(count * own, wide_chans)
        grad = dot(mine(ext_h, r0, count), flat, TN)
        parts = [grad[:, k * chans : (k + 1) * chans] for k in range(basis)]
        keep_grad(1, jnp.concatenate(parts, 0), first)
        flat = y1[pl.ds(r0, count)].reshape(count * own, wide_chans)
        keep_grad(0, dot(flat, mine(ext_d, r0, count), TN), first)

    def halves(field, ext, body, between=None):
        for part in range(2):
            arrive(halo(field, ext, (part,)))
            lax.fori_loop(part * nblk // 2, (part + 1) * nblk // 2, body, 0)
            if between is not None:
                between(part)

    sent(halo(0, ext_f))
    start(halo(1, ext_c))
    halves(0, ext_f, first)
    sent(halo(1, ext_c))
    start(halo(2, ext_h))

    arrive(tap_copies())
    for k in range(basis):
        tap = jnp.where(lat > 0, edge_in[0, pl.ds(k * 3 + 2, 1)], 0.0)
        back[1, pl.ds(k * own, own), pl.ds(0, WIDE)] = toeplitz(tap)
        tap = jnp.where(lat < nlat - 1, edge_in[1, pl.ds(k * 3, 1)], 0.0)
        back[rows, pl.ds(k * own, own), pl.ds(2 * WIDE, WIDE)] = toeplitz(tap)
    halves(
        1,
        ext_c,
        first_back,
        lambda part: weight_grads(part * (rows // 2), rows // 2, part == 0),
    )
    gb[...] = p32[1 - my_core].astype(BF)
    start([core_scatter(d) for d in far_first + [0]])
    reduce_core()
    sent(halo(2, ext_h))
    start(halo(3, ext_d))

    halves(2, ext_h, second)
    emit(0, out_ref)
    reduce_x()
    reduce_y()
    halves(3, ext_d, second_back, lambda part: reduce_z() if part == 0 else None)
    gather_z()
    emit(1, gin_ref)
    gather_y()
    gather_x()
    last = pltpu.make_async_copy(gfull, grad_ref, out_sem.at[2])
    last.start()

    sent(halo(3, ext_d) + tap_copies())
    sent([make(d) for make in (core_scatter, core_gather) for d in range(nx)])
    sent(every(x_scatter, nx) + every(x_gather, nx))
    sent(every(y_scatter, ny) + every(y_gather, ny))
    sent(every(z_scatter, nz) + every(z_gather, nz))
    outgoing(0, out_ref).wait()
    outgoing(1, gin_ref).wait()
    last.wait()


def deliver(nx, half, out_in, gin_in, grad_in, out_ref, gin_ref, g1_ref, g2_ref, *scratch):
    out, gin, grad, g1, g2, in_sems, out_sems = scratch
    cells = out.shape[0]
    cut = cells // 2

    def put(i, src, dst, sems):
        return pltpu.make_async_copy(src, dst, sems.at[i])

    steps = [(4, grad_in, grad)]
    for i, (src, dst) in enumerate([(out_in, out), (gin_in, gin)]):
        steps += [(2 * i + j, src.at[at], dst.at[at]) for j, at in enumerate(parts_of(cells, cut))]
    arriving = [put(i, src, dst, in_sems) for i, src, dst in steps]
    for copy in arriving:
        copy.start()
    arriving[0].wait()
    for core in range(2):
        for x in range(nx):
            at = pl.ds((core * nx + x) * half, half)
            flat = grad[core, x].reshape(2 * half, grad.shape[-1]).astype(F32)
            g1[at] = flat[:half]
            g2[at] = flat[half:]
    leaving = [put(4, g1, g1_ref, out_sems), put(5, g2, g2_ref, out_sems)]
    for copy in leaving:
        copy.start()
    for i, (src, dst) in enumerate([(out, out_ref), (gin, gin_ref)]):
        for j, at in enumerate(parts_of(cells, cut)):
            arriving[1 + 2 * i + j].wait()
            copy = put(2 * i + j, src.at[at], dst.at[at], out_sems)
            copy.start()
            leaving.append(copy)
    for copy in leaving:
        copy.wait()


def parts_of(count, cut):
    return pl.ds(0, cut), pl.ds(cut, count - cut)


def local(sizes, features, cotangent, basis, support, weight_one, weight_two):
    nx, nyl, nz, nyh = sizes
    rows, cols, chans = features.shape
    count = weight_one.shape[0]
    nlat, nlon = nx * nyl * 2, nz * nyh
    ny = nyl * nyh
    scaling = 1.0 / math.sqrt(rows * nlat * cols * nlon)
    own = -(-cols // 16) * 16
    chunk = count * chans // nx
    slab = chunk // ny
    piece = slab // nz

    vmem = pl.BlockSpec(memory_space=pltpu.VMEM)
    smem = pl.BlockSpec(memory_space=pltpu.SMEM)
    hbm = pl.BlockSpec(memory_space=pl.ANY)
    dma = pltpu.SemaphoreType.DMA
    ext = pltpu.VMEM((rows + 2, WIDE, chans), BF)
    field = jax.ShapeDtypeStruct((cols, rows, chans), BF)
    out, gin, grads = pl.pallas_call(
        functools.partial(kernel, (nx, nyl, nz, nyh, rows, cols, chans, count, scaling)),
        out_shape=(field, field, jax.ShapeDtypeStruct((2, nx, ny, slab, chans), BF)),
        in_specs=[hbm, hbm, vmem, smem, hbm, hbm],
        out_specs=(hbm,) * 3,
        scratch_shapes=[
            pltpu.VMEM((own, rows, chans), BF),
            pltpu.VMEM((own, rows, chans), BF),
            pltpu.VMEM((count, chans, chans), BF),
            pltpu.VMEM((count, chans, chans), BF),
            pltpu.VMEM((count, chans, chans), BF),
            pltpu.VMEM((count, chans, chans), BF),
            pltpu.VMEM((HW * HW, HW * HW), BF),
            ext,
            ext,
            ext,
            ext,
            pltpu.VMEM((4, rows, HW, chans), BF),
            pltpu.VMEM((count * 3, rows, WIDE), F32),
            pltpu.VMEM((rows, count * 3, 2 * WIDE), F32),
            pltpu.VMEM((2, count * 3, WIDE), F32),
            pltpu.VMEM((2, count * 3, WIDE), F32),
            pltpu.VMEM((rows, count * own, 3 * WIDE), BF),
            pltpu.VMEM((rows + 2, count * own, 3 * WIDE), BF),
            pltpu.VMEM((rows, own, count * chans), BF),
            pltpu.VMEM((rows, own, count * chans), BF),
            pltpu.VMEM((rows, own, count * chans), BF),
            pltpu.VMEM((rows, own, chans), F32),
            pltpu.VMEM((2, rows, own, chans), BF),
            pltpu.VMEM((2, own, rows, chans), BF),
            pltpu.VMEM((2, nx, chunk, chans), F32),
            pltpu.VMEM((nx, chunk, chans), BF),
            pltpu.VMEM((nx, chunk, chans), BF),
            pltpu.VMEM((nx, chunk, chans), BF),
            pltpu.VMEM((nx - 1, chunk, chans), BF),
            pltpu.VMEM((ny, slab, chans), F32),
            pltpu.VMEM((ny, slab, chans), BF),
            pltpu.VMEM((ny - 1, slab, chans), BF),
            pltpu.VMEM((nz, piece, chans), F32),
            pltpu.VMEM((nz - 1, piece, chans), F32),
            pltpu.VMEM((nz, piece, chans), F32),
            pltpu.VMEM((slab, chans), F32),
            pltpu.VMEM((2, nx, ny, slab, chans), BF),
            dma((4,)),
            dma((3,)),
            dma((4, 2, 5)),
            dma((4, 2, 5)),
            dma((2,)),
            dma((2,)),
            dma((2, nx)),
            dma((2, nx)),
            dma((2, nx)),
            dma((2, nx)),
            dma((2, ny)),
            dma((2, ny)),
            dma((2, nz)),
            dma((2, nz)),
        ],
        compiler_params=pltpu.CompilerParams(
            collective_id=0, has_side_effects=True, vmem_limit_bytes=60 * 1024 * 1024
        ),
    )(
        features.transpose(1, 0, 2),
        cotangent.transpose(1, 0, 2),
        basis.transpose(1, 2, 0, 3),
        support,
        weight_one,
        weight_two,
    )
    weights = jax.ShapeDtypeStruct((count * chans, chans), F32)
    out, gin, g1, g2 = pl.pallas_call(
        functools.partial(deliver, nx, chunk // 2),
        out_shape=(field, field, weights, weights),
        in_specs=[hbm] * 3,
        out_specs=(hbm,) * 4,
        scratch_shapes=[
            pltpu.VMEM(field.shape, BF),
            pltpu.VMEM(field.shape, BF),
            pltpu.VMEM(grads.shape, BF),
            pltpu.VMEM(weights.shape, F32),
            pltpu.VMEM(weights.shape, F32),
            dma((5,)),
            dma((6,)),
        ],
        compiler_params=pltpu.CompilerParams(vmem_limit_bytes=60 * 1024 * 1024),
    )(out, gin, grads)
    shape = weight_one.shape
    return out.transpose(1, 0, 2), gin.transpose(1, 0, 2), g1.reshape(shape), g2.reshape(shape)


def solution(mesh):
    nlat, nlon = mesh.shape["lat"], mesh.shape["lon"]
    nyl = 2 if nlat >= 16 else 1
    sizes = (nlat // (2 * nyl), nyl, nlon // 2, 2)
    placed = (
        P("lat", "lon", None),
        P("lat", "lon", None),
        P("lat", None, None, None),
        P("lat"),
        P(),
        P(),
    )
    return jax.shard_map(
        functools.partial(local, sizes),
        mesh=mesh,
        in_specs=placed,
        out_specs=(P("lat", "lon", None), P("lat", "lon", None), P(), P()),
        check_vma=False,
    )
```

```python
import functools
import math

import jax
import jax.numpy as jnp
from jax import lax
from jax.experimental import pallas as pl
from jax.experimental.pallas import tpu as pltpu
from jax.sharding import PartitionSpec as P

HW = 16
SPAN = 2 * HW + 1
WIDE = 128
MESH = pl.DeviceIdType.MESH
BF = jnp.bfloat16
F32 = jnp.float32
NN = (((1,), (0,)), ((), ()))
NT = (((1,), (1,)), ((), ()))
TN = (((0,), (0,)), ((), ()))


def dot(a, b, dims=NN):
    return lax.dot_general(a, b, dims, preferred_element_type=F32)


def iota(shape, dim):
    return lax.broadcasted_iota(jnp.int32, shape, dim)


def kernel(
    dims,
    f_ref,
    c_ref,
    basis_ref,
    support_ref,
    w1_ref,
    w2_ref,
    out_ref,
    gin_ref,
    grad_ref,
    raw_f,
    raw_c,
    w1,
    w2,
    w1t,
    w2t,
    perm,
    ext_f,
    ext_c,
    ext_h,
    ext_d,
    tails,
    loose,
    taps,
    edge_out,
    edge_in,
    band,
    back,
    y1,
    v2,
    tmp,
    dsig,
    natural,
    turned,
    p32,
    gb,
    r1,
    sb,
    r2,
    zall,
    gfull,
    in_sem,
    out_sem,
    halo_snd,
    halo_rcv,
    tap_snd,
    tap_rcv,
    core_snd,
    core_rcv,
    xy_snd,
    xy_rcv,
    z_snd,
    z_rcv,
):
    nx, nyl, nz, nyh, rows, cols, chans, basis, scaling = dims
    own = -(-cols // 16) * 16
    right = own
    left = WIDE - HW
    nlat, nlon = nx * nyl * 2, nz * nyh
    ny = nyl * nyh
    blk = 4
    nblk = rows // blk
    wide_chans = basis * chans

    inputs = [
        pltpu.make_async_copy(src, dst, in_sem.at[i])
        for i, (src, dst) in enumerate(
            [
                (f_ref, raw_f.at[pl.ds(0, cols)]),
                (c_ref, raw_c.at[pl.ds(0, cols)]),
                (w1_ref, w1),
                (w2_ref, w2),
            ]
        )
    ]
    for copy in inputs:
        copy.start()

    lat = lax.axis_index("lat")
    lon = lax.axis_index("lon")

    def wrap(value, count):
        return jnp.where(value >= count, value - count, value)

    my_x = lat // (nyl * 2)
    in_x = lat - my_x * (nyl * 2)
    my_yl = in_x // 2
    my_core = in_x - my_yl * 2
    my_z = lon // nyh
    my_y = (lon - my_z * nyh) * nyl + my_yl
    north, south = wrap(lat + nlat - 1, nlat), wrap(lat + 1, nlat)
    west, east = wrap(lon + nlon - 1, nlon), wrap(lon + 1, nlon)

    partner = (lat + 1 - 2 * my_core, lon)
    around = [
        (lat, east),
        (lat, west),
        (south, lon),
        (north, lon),
        (south, east),
        (north, east),
        (south, west),
        (north, west),
    ]
    x_peers = [wrap(my_x + d, nx) for d in range(nx)]
    x_from = [wrap(my_x + nx - d, nx) for d in range(nx)]
    y_peers = [wrap(my_y + d, ny) for d in range(ny)]
    z_peers = [wrap(my_z + d, nz) for d in range(nz)]
    my_yh = lon - my_z * nyh
    xy_devices = {}
    for dy, y in enumerate(y_peers):
        yh = y // nyl
        for dx, x in enumerate(x_peers):
            to = (x * (nyl * 2) + (y - yh * nyl) * 2 + my_core, my_z * nyh + yh)
            xy_devices[dx, dy] = to
    z_devices = [(lat, z * nyh + my_yh) for z in z_peers]

    barrier = pltpu.get_barrier_semaphore()

    def greet(device):
        pl.semaphore_signal(barrier, inc=1, device_id=device, device_id_type=MESH)

    for device in around:
        greet(device)
    others = z_devices[1:] + list(xy_devices.values())[1:] + [partner]
    for device in others:
        greet(device)

    side = HW * HW
    i0, i1 = iota((side, side), 0), iota((side, side), 1)
    perm[...] = jnp.where(i1 == (i0 & 15) * HW + (i0 >> 4), 1.0, 0.0).astype(BF)

    def turn(block):
        return dot(perm[...], block.reshape(side, chans)).astype(BF).reshape(HW, HW, chans)

    def stage(field, raw, ext):
        raw[pl.ds(cols, own - cols)] = jnp.zeros((own - cols, rows, chans), BF)
        tails[field] = turn(raw[pl.ds(cols - HW, HW)])
        for b in range(own // HW):
            ext[pl.ds(1, rows), pl.ds(b * HW, HW)] = turn(raw[pl.ds(b * HW, HW)])

    def remote(src, dst, snd, rcv, device):
        return pltpu.make_async_remote_copy(
            src_ref=src,
            dst_ref=dst,
            send_sem=snd,
            recv_sem=rcv,
            device_id=device,
            device_id_type=MESH,
        )

    def halo(field, ext, parts=(0, 1)):
        tail = tails.at[field]
        top = rows // 2 + 1
        upper, lower = pl.ds(1, top), pl.ds(1 + top, rows - top)
        moves = [
            [
                (tail.at[pl.ds(0, top)], ext.at[upper, pl.ds(left, HW)], 0),
                (ext.at[upper, pl.ds(0, HW)], ext.at[upper, pl.ds(right, HW)], 1),
                (ext.at[rows, pl.ds(0, own)], ext.at[0, pl.ds(0, own)], 2),
                (tail.at[rows - 1], ext.at[0, pl.ds(left, HW)], 4),
                (ext.at[rows, pl.ds(0, HW)], ext.at[0, pl.ds(right, HW)], 6),
            ],
            [
                (tail.at[pl.ds(top, rows - top)], ext.at[lower, pl.ds(left, HW)], 0),
                (ext.at[lower, pl.ds(0, HW)], ext.at[lower, pl.ds(right, HW)], 1),
                (ext.at[1, pl.ds(0, own)], ext.at[rows + 1, pl.ds(0, own)], 3),
                (tail.at[0], ext.at[rows + 1, pl.ds(left, HW)], 5),
                (ext.at[1, pl.ds(0, HW)], ext.at[rows + 1, pl.ds(right, HW)], 7),
            ],
        ]
        return [
            remote(src, dst, halo_snd.at[field, part, i], halo_rcv.at[field, part, i], around[to])
            for part in parts
            for i, (src, dst, to) in enumerate(moves[part])
        ]

    def tap_copies():
        return [
            remote(edge_out.at[i], edge_in.at[i], tap_snd.at[i], tap_rcv.at[i], device)
            for i, device in enumerate([(south, lon), (north, lon)])
        ]

    def start(copies):
        for copy in copies:
            copy.start()

    def arrive(copies):
        for copy in copies:
            copy.wait_recv()

    def sent(copies):
        for copy in copies:
            copy.wait_send()

    inputs[0].wait()
    stage(0, raw_f, ext_f)
    pl.semaphore_wait(barrier, len(around) + len(others))
    start(halo(0, ext_f))

    loose[...] = jnp.zeros(loose.shape, F32)
    row = iota((rows, WIDE), 0)
    lane = iota((rows, WIDE), 1)
    reach = jnp.zeros((rows, WIDE), jnp.int32)
    for r in range(rows):
        reach = jnp.where(row == r, support_ref[r], reach)
    inside = jnp.abs(lane - HW) <= reach
    for k in range(basis):
        for a in range(3):
            loose[k * 3 + a, :, pl.ds(0, SPAN)] = basis_ref[k, a].astype(F32)
    b0, b1 = iota((WIDE, 2 * WIDE), 0), iota((WIDE, 2 * WIDE), 1)
    place = (b1 == ((b0 - HW) & (WIDE - 1))) | (b1 == ((HW - b0) & (WIDE - 1)) + WIDE)
    place = jnp.where(place, 1.0, 0.0).astype(BF)
    for k in range(basis):
        for a in range(3):
            ka = k * 3 + a
            masked = jnp.where(inside, loose[ka], 0.0).astype(BF)
            placed = dot(masked, place)
            edge_out[0, pl.ds(ka, 1)] = placed[rows - 1 : rows, WIDE:]
            edge_out[1, pl.ds(ka, 1)] = placed[:1, WIDE:]
            forward = placed[:, :WIDE]
            if a == 0:
                forward = jnp.where((row == 0) & (lat == 0), 0.0, forward)
            elif a == 2:
                forward = jnp.where((row == rows - 1) & (lat == nlat - 1), 0.0, forward)
            for r in range(rows):
                taps[r, pl.ds(ka, 1), pl.ds(0, WIDE)] = forward[r : r + 1]
                taps[r, pl.ds(ka, 1), pl.ds(WIDE, WIDE)] = placed[r : r + 1, WIDE:]
    start(tap_copies())

    low_tiles = [own - 2 * HW, own - HW]
    at = iota((HW, WIDE), 1)
    plain, moved = [], []
    for j in low_tiles:
        valid = iota((HW, WIDE), 0) + j < cols
        plain.append(valid & ((at < cols) | (at >= left)))
        moved.append(valid & (at >= right) & (at < left))
    gap = own - cols

    def toeplitz(tap):
        wide = jnp.broadcast_to(tap, (HW, WIDE))
        tile = pltpu.roll(wide, 0, 1, stride=1, stride_axis=0).astype(BF)
        tiles = [tile] + [pltpu.roll(tile, j, 1) for j in range(HW, own, HW)]
        for i, j in enumerate(low_tiles):
            shifted = pltpu.roll(tile, j + gap, 1)
            tiles[j // HW] = jnp.where(moved[i], shifted, jnp.where(plain[i], tiles[j // HW], 0))
        return jnp.concatenate(tiles, axis=0)

    def build_fwd(r, carry):
        for k in range(basis):
            for a in range(3):
                tap = taps[r, pl.ds(k * 3 + a, 1), pl.ds(0, WIDE)]
                band[r, pl.ds(k * own, own), pl.ds(a * WIDE, WIDE)] = toeplitz(tap)
        return carry

    def build_back(r, carry):
        for k in range(basis):
            for a in range(3):
                tap = taps[r, pl.ds(k * 3 + a, 1), pl.ds(WIDE, WIDE)]
                t = 2 - a
                back[r + a, pl.ds(k * own, own), pl.ds(t * WIDE, WIDE)] = toeplitz(tap)
        return carry

    lax.fori_loop(0, rows, build_fwd, 0)

    inputs[1].wait()
    stage(1, raw_c, ext_c)
    inputs[2].wait()
    inputs[3].wait()
    eye = jnp.where(iota((chans, chans), 0) == iota((chans, chans), 1), 1.0, 0.0).astype(BF)
    for k in range(basis):
        w1t[k] = dot(eye, w1[k], NT).astype(BF)
        w2t[k] = dot(eye, w2[k], NT).astype(BF)
    lax.fori_loop(0, rows, build_back, 0)

    def stencil(ext, matrix, at, y, r):
        x = ext[pl.ds(r, 3)].reshape(3 * WIDE, chans)
        t = dot(matrix[r + at], x).astype(BF)
        for k in range(basis):
            y[r, :, pl.ds(k * chans, chans)] = t[k * own : (k + 1) * own]

    def convolve(ext, matrix, at, y, w, r0):
        for i in range(blk):
            stencil(ext, matrix, at, y, r0 + i)
        flat = y[pl.ds(r0, blk)].reshape(blk * own, wide_chans)
        return dot(flat, w[...].reshape(wide_chans, chans))

    def put(field, ext, r0, value):
        value = value.reshape(blk, own, chans)
        ext[pl.ds(r0 + 1, blk), pl.ds(0, own)] = value.astype(BF)
        for i in range(blk):
            tails[field, r0 + i] = value[i, cols - HW : cols].astype(BF)

    def first(b, carry):
        r0 = b * blk
        z = convolve(ext_f, band, 0, y1, w1, r0)
        sigma = jax.nn.sigmoid(z)
        dsig[pl.ds(r0, blk)] = (sigma * (1.0 + z * (1.0 - sigma))).reshape(blk, own, chans)
        put(2, ext_h, r0, z * sigma)
        return carry

    def first_back(b, carry):
        r0 = b * blk
        g = convolve(ext_c, back, 1, v2, w2t, r0)
        put(3, ext_d, r0, g * dsig[pl.ds(r0, blk)].reshape(blk * own, chans))
        return carry

    def second(b, carry):
        r0 = b * blk
        z = convolve(ext_h, band, 0, tmp, w2, r0)
        natural[0, pl.ds(r0, blk)] = z.astype(BF).reshape(blk, own, chans)
        return carry

    def second_back(b, carry):
        r0 = b * blk
        z = convolve(ext_d, back, 1, tmp, w1t, r0)
        natural[1, pl.ds(r0, blk)] = z.astype(BF).reshape(blk, own, chans)
        return carry

    def outgoing(i, ref):
        return pltpu.make_async_copy(turned.at[i, pl.ds(0, cols)], ref, out_sem.at[i])

    def emit(i, ref):
        for b in range(own // HW):
            turned[i, pl.ds(b * HW, HW)] = turn(natural[i, :, pl.ds(b * HW, HW)])
        outgoing(i, ref).start()

    chunk = wide_chans // nx
    half = chunk // 2
    slab = chunk // ny
    far_first = sorted(range(nx), key=lambda d: -min(d, nx - d))
    near_first = far_first[::-1]
    far_first_y = sorted(range(ny), key=lambda d: -min(d, ny - d))

    def core_scatter(d):
        x = x_peers[d]
        return remote(gb.at[x], r1.at[x], core_snd.at[0, d], core_rcv.at[0, d], partner)

    def xy_scatter(dx, dy):
        i = dx * ny + dy
        src = sb.at[x_peers[dx], y_peers[dy]]
        return remote(src, r2.at[i], xy_snd.at[0, i], xy_rcv.at[0, i], xy_devices[dx, dy])

    def z_spread(d):
        own_slab = zall.at[my_z]
        return remote(own_slab, own_slab, z_snd.at[d], z_rcv.at[d], z_devices[d])

    def xy_gather(dx, dy):
        i = dx * ny + dy
        own_slab = gfull.at[my_core, my_x, my_y]
        return remote(own_slab, own_slab, xy_snd.at[1, i], xy_rcv.at[1, i], xy_devices[dx, dy])

    def core_gather(d):
        arrived = gfull.at[my_core, x_from[d]]
        return remote(arrived, arrived, core_snd.at[1, d], core_rcv.at[1, d], partner)

    xy_order = [(dx, dy) for dx in far_first for dy in far_first_y if dx + dy > 0]

    def keep_grad(g, value, first):
        for core in range(2):
            for x in range(nx):
                at = (core * nx + x) * half
                to = (core, x, pl.ds(g * half, half))
                share = value[at : at + half]
                p32[to] = share if first else p32[to] + share

    def reduce_core():
        for dx in far_first:
            x = x_peers[dx]
            core_scatter(dx).wait_recv()
            total = p32[my_core, x].reshape(ny, slab, chans) + r1[x].astype(F32)
            sb[x] = total.astype(BF)
            start([xy_scatter(*to) for to in xy_order if to[0] == dx])

    def reduce_xy():
        total = p32[my_core, my_x, pl.ds(pl.multiple_of(my_y * slab, slab), slab)]
        total = total + r1[my_x, my_y].astype(F32)
        for to in xy_order[::-1]:
            xy_scatter(*to).wait_recv()
            total = total + r2[to[0] * ny + to[1]].astype(F32)
        zall[my_z] = total.astype(BF)
        start([z_spread(d) for d in sorted(range(1, nz), key=lambda d: -min(d, nz - d))])

    def reduce_z():
        arrive([z_spread(d) for d in range(1, nz)])
        total = zall[0].astype(F32)
        for z in range(1, nz):
            total = total + zall[z].astype(F32)
        gfull[my_core, my_x, my_y] = (total * scaling).astype(BF)
        start([xy_gather(*to) for to in xy_order])

    def gather_xy():
        for dx in near_first:
            arrive([xy_gather(*to) for to in xy_order if to[0] == dx])
            core_gather(dx).start()

    def gather_core():
        arrive([core_gather(d) for d in range(nx)])

    def mine(ext, r0, count):
        return ext[pl.ds(r0 + 1, count), pl.ds(0, own)].reshape(count * own, chans)

    def weight_grads(r0, count, first):
        flat = v2[pl.ds(r0, count)].reshape(count * own, wide_chans)
        grad = dot(mine(ext_h, r0, count), flat, TN)
        parts = [grad[:, k * chans : (k + 1) * chans] for k in range(basis)]
        keep_grad(1, jnp.concatenate(parts, 0), first)
        flat = y1[pl.ds(r0, count)].reshape(count * own, wide_chans)
        keep_grad(0, dot(flat, mine(ext_d, r0, count), TN), first)

    def halves(field, ext, body, between=None):
        for part in range(2):
            arrive(halo(field, ext, (part,)))
            lax.fori_loop(part * nblk // 2, (part + 1) * nblk // 2, body, 0)
            if between is not None:
                between(part)

    sent(halo(0, ext_f))
    start(halo(1, ext_c))
    halves(0, ext_f, first)
    sent(halo(1, ext_c))
    start(halo(2, ext_h))

    arrive(tap_copies())
    for k in range(basis):
        tap = jnp.where(lat > 0, edge_in[0, pl.ds(k * 3 + 2, 1)], 0.0)
        back[1, pl.ds(k * own, own), pl.ds(0, WIDE)] = toeplitz(tap)
        tap = jnp.where(lat < nlat - 1, edge_in[1, pl.ds(k * 3, 1)], 0.0)
        back[rows, pl.ds(k * own, own), pl.ds(2 * WIDE, WIDE)] = toeplitz(tap)
    halves(
        1,
        ext_c,
        first_back,
        lambda part: weight_grads(part * (rows // 2), rows // 2, part == 0),
    )
    gb[...] = p32[1 - my_core].astype(BF).reshape(gb.shape)
    start([core_scatter(d) for d in far_first])
    reduce_core()
    halves(2, ext_h, second)
    reduce_xy()
    sent(halo(2, ext_h))
    start(halo(3, ext_d))
    emit(0, out_ref)
    reduce_z()
    halves(3, ext_d, second_back)
    emit(1, gin_ref)
    gather_xy()
    gather_core()
    last = pltpu.make_async_copy(gfull, grad_ref, out_sem.at[2])
    last.start()

    sent(halo(3, ext_d) + tap_copies())
    sent([make(d) for make in (core_scatter, core_gather) for d in range(nx)])
    sent([make(*to) for make in (xy_scatter, xy_gather) for to in xy_order])
    sent([z_spread(d) for d in range(1, nz)])
    outgoing(0, out_ref).wait()
    outgoing(1, gin_ref).wait()
    last.wait()


def deliver(nx, half, out_in, gin_in, grad_in, out_ref, gin_ref, g1_ref, g2_ref, *scratch):
    out, gin, grad, g1, g2, in_sems, out_sems = scratch
    cells = out.shape[0]
    cut = cells // 2

    def put(i, src, dst, sems):
        return pltpu.make_async_copy(src, dst, sems.at[i])

    steps = [(4, grad_in, grad)]
    for i, (src, dst) in enumerate([(out_in, out), (gin_in, gin)]):
        steps += [(2 * i + j, src.at[at], dst.at[at]) for j, at in enumerate(parts_of(cells, cut))]
    arriving = [put(i, src, dst, in_sems) for i, src, dst in steps]
    for copy in arriving:
        copy.start()
    arriving[0].wait()
    for core in range(2):
        for x in range(nx):
            at = pl.ds((core * nx + x) * half, half)
            flat = grad[core, x].reshape(2 * half, grad.shape[-1]).astype(F32)
            g1[at] = flat[:half]
            g2[at] = flat[half:]
    leaving = [put(4, g1, g1_ref, out_sems), put(5, g2, g2_ref, out_sems)]
    for copy in leaving:
        copy.start()
    for i, (src, dst) in enumerate([(out, out_ref), (gin, gin_ref)]):
        for j, at in enumerate(parts_of(cells, cut)):
            arriving[1 + 2 * i + j].wait()
            copy = put(2 * i + j, src.at[at], dst.at[at], out_sems)
            copy.start()
            leaving.append(copy)
    for copy in leaving:
        copy.wait()


def parts_of(count, cut):
    return pl.ds(0, cut), pl.ds(cut, count - cut)


def local(sizes, features, cotangent, basis, support, weight_one, weight_two):
    nx, nyl, nz, nyh = sizes
    rows, cols, chans = features.shape
    count = weight_one.shape[0]
    nlat, nlon = nx * nyl * 2, nz * nyh
    ny = nyl * nyh
    scaling = 1.0 / math.sqrt(rows * nlat * cols * nlon)
    own = -(-cols // 16) * 16
    chunk = count * chans // nx
    slab = chunk // ny

    vmem = pl.BlockSpec(memory_space=pltpu.VMEM)
    smem = pl.BlockSpec(memory_space=pltpu.SMEM)
    hbm = pl.BlockSpec(memory_space=pl.ANY)
    dma = pltpu.SemaphoreType.DMA
    ext = pltpu.VMEM((rows + 2, WIDE, chans), BF)
    field = jax.ShapeDtypeStruct((cols, rows, chans), BF)
    out, gin, grads = pl.pallas_call(
        functools.partial(kernel, (nx, nyl, nz, nyh, rows, cols, chans, count, scaling)),
        out_shape=(field, field, jax.ShapeDtypeStruct((2, nx, ny, slab, chans), BF)),
        in_specs=[hbm, hbm, vmem, smem, hbm, hbm],
        out_specs=(hbm,) * 3,
        scratch_shapes=[
            pltpu.VMEM((own, rows, chans), BF),
            pltpu.VMEM((own, rows, chans), BF),
            pltpu.VMEM((count, chans, chans), BF),
            pltpu.VMEM((count, chans, chans), BF),
            pltpu.VMEM((count, chans, chans), BF),
            pltpu.VMEM((count, chans, chans), BF),
            pltpu.VMEM((HW * HW, HW * HW), BF),
            ext,
            ext,
            ext,
            ext,
            pltpu.VMEM((4, rows, HW, chans), BF),
            pltpu.VMEM((count * 3, rows, WIDE), F32),
            pltpu.VMEM((rows, count * 3, 2 * WIDE), F32),
            pltpu.VMEM((2, count * 3, WIDE), F32),
            pltpu.VMEM((2, count * 3, WIDE), F32),
            pltpu.VMEM((rows, count * own, 3 * WIDE), BF),
            pltpu.VMEM((rows + 2, count * own, 3 * WIDE), BF),
            pltpu.VMEM((rows, own, count * chans), BF),
            pltpu.VMEM((rows, own, count * chans), BF),
            pltpu.VMEM((rows, own, count * chans), BF),
            pltpu.VMEM((rows, own, chans), F32),
            pltpu.VMEM((2, rows, own, chans), BF),
            pltpu.VMEM((2, own, rows, chans), BF),
            pltpu.VMEM((2, nx, chunk, chans), F32),
            pltpu.VMEM((nx, ny, slab, chans), BF),
            pltpu.VMEM((nx, ny, slab, chans), BF),
            pltpu.VMEM((nx, ny, slab, chans), BF),
            pltpu.VMEM((nx * ny, slab, chans), BF),
            pltpu.VMEM((nz, slab, chans), BF),
            pltpu.VMEM((2, nx, ny, slab, chans), BF),
            dma((4,)),
            dma((3,)),
            dma((4, 2, 5)),
            dma((4, 2, 5)),
            dma((2,)),
            dma((2,)),
            dma((2, nx)),
            dma((2, nx)),
            dma((2, nx * ny)),
            dma((2, nx * ny)),
            dma((nz,)),
            dma((nz,)),
        ],
        compiler_params=pltpu.CompilerParams(
            collective_id=0, has_side_effects=True, vmem_limit_bytes=60 * 1024 * 1024
        ),
    )(
        features.transpose(1, 0, 2),
        cotangent.transpose(1, 0, 2),
        basis.transpose(1, 2, 0, 3),
        support,
        weight_one,
        weight_two,
    )
    weights = jax.ShapeDtypeStruct((count * chans, chans), F32)
    out, gin, g1, g2 = pl.pallas_call(
        functools.partial(deliver, nx, chunk // 2),
        out_shape=(field, field, weights, weights),
        in_specs=[hbm] * 3,
        out_specs=(hbm,) * 4,
        scratch_shapes=[
            pltpu.VMEM(field.shape, BF),
            pltpu.VMEM(field.shape, BF),
            pltpu.VMEM(grads.shape, BF),
            pltpu.VMEM(weights.shape, F32),
            pltpu.VMEM(weights.shape, F32),
            dma((5,)),
            dma((6,)),
        ],
        compiler_params=pltpu.CompilerParams(vmem_limit_bytes=60 * 1024 * 1024),
    )(out, gin, grads)
    shape = weight_one.shape
    return out.transpose(1, 0, 2), gin.transpose(1, 0, 2), g1.reshape(shape), g2.reshape(shape)


def solution(mesh):
    nlat, nlon = mesh.shape["lat"], mesh.shape["lon"]
    nyl = 2 if nlat >= 16 else 1
    sizes = (nlat // (2 * nyl), nyl, nlon // 2, 2)
    placed = (
        P("lat", "lon", None),
        P("lat", "lon", None),
        P("lat", None, None, None),
        P("lat"),
        P(),
        P(),
    )
    return jax.shard_map(
        functools.partial(local, sizes),
        mesh=mesh,
        in_specs=placed,
        out_specs=(P("lat", "lon", None), P("lat", "lon", None), P(), P()),
        check_vma=False,
    )
```

```python
import functools
import math

import jax
import jax.numpy as jnp
from jax import lax
from jax.experimental import pallas as pl
from jax.experimental.pallas import tpu as pltpu
from jax.sharding import PartitionSpec as P

HW = 16
SPAN = 2 * HW + 1
WIDE = 128
MESH = pl.DeviceIdType.MESH
BF = jnp.bfloat16
F32 = jnp.float32
NN = (((1,), (0,)), ((), ()))
NT = (((1,), (1,)), ((), ()))
TN = (((0,), (0,)), ((), ()))


def dot(a, b, dims=NN):
    return lax.dot_general(a, b, dims, preferred_element_type=F32)


def iota(shape, dim):
    return lax.broadcasted_iota(jnp.int32, shape, dim)


def kernel(
    dims,
    f_ref,
    c_ref,
    basis_ref,
    support_ref,
    w1_ref,
    w2_ref,
    out_ref,
    gin_ref,
    grad_ref,
    raw_f,
    raw_c,
    w1,
    w2,
    w1t,
    w2t,
    perm,
    ext_f,
    ext_c,
    ext_h,
    ext_d,
    tails,
    loose,
    taps,
    edge_out,
    edge_in,
    band,
    back,
    y1,
    v2,
    tmp,
    dsig,
    natural,
    turned,
    p32,
    gb,
    r1,
    sb,
    r2,
    zall,
    gfull,
    in_sem,
    out_sem,
    halo_snd,
    halo_rcv,
    tap_snd,
    tap_rcv,
    core_snd,
    core_rcv,
    xy_snd,
    xy_rcv,
    z_snd,
    z_rcv,
):
    nx, nyl, nz, nyh, rows, cols, chans, basis, scaling = dims
    own = -(-cols // 16) * 16
    right = own
    left = WIDE - HW
    nlat, nlon = nx * nyl * 2, nz * nyh
    ny = nyl * nyh
    blk = 4
    nblk = rows // blk
    wide_chans = basis * chans

    inputs = [
        pltpu.make_async_copy(src, dst, in_sem.at[i])
        for i, (src, dst) in enumerate(
            [
                (f_ref, raw_f.at[pl.ds(0, cols)]),
                (c_ref, raw_c.at[pl.ds(0, cols)]),
                (w1_ref, w1),
                (w2_ref, w2),
            ]
        )
    ]
    for copy in inputs:
        copy.start()

    lat = lax.axis_index("lat")
    lon = lax.axis_index("lon")

    def wrap(value, count):
        return jnp.where(value >= count, value - count, value)

    my_x = lat // (nyl * 2)
    in_x = lat - my_x * (nyl * 2)
    my_yl = in_x // 2
    my_core = in_x - my_yl * 2
    my_z = lon // nyh
    my_y = (lon - my_z * nyh) * nyl + my_yl
    north, south = wrap(lat + nlat - 1, nlat), wrap(lat + 1, nlat)
    west, east = wrap(lon + nlon - 1, nlon), wrap(lon + 1, nlon)

    partner = (lat + 1 - 2 * my_core, lon)
    around = [
        (lat, east),
        (lat, west),
        (south, lon),
        (north, lon),
        (south, east),
        (north, east),
        (south, west),
        (north, west),
    ]
    x_peers = [wrap(my_x + d, nx) for d in range(nx)]
    x_from = [wrap(my_x + nx - d, nx) for d in range(nx)]
    y_peers = [wrap(my_y + d, ny) for d in range(ny)]
    z_peers = [wrap(my_z + d, nz) for d in range(nz)]
    my_yh = lon - my_z * nyh
    xy_devices = {}
    for dy, y in enumerate(y_peers):
        yh = y // nyl
        for dx, x in enumerate(x_peers):
            to = (x * (nyl * 2) + (y - yh * nyl) * 2 + my_core, my_z * nyh + yh)
            xy_devices[dx, dy] = to
    z_devices = [(lat, z * nyh + my_yh) for z in z_peers]

    barrier = pltpu.get_barrier_semaphore()

    def greet(device):
        pl.semaphore_signal(barrier, inc=1, device_id=device, device_id_type=MESH)

    for device in around:
        greet(device)
    others = z_devices[1:] + list(xy_devices.values())[1:] + [partner]
    for device in others:
        greet(device)

    side = HW * HW
    i0, i1 = iota((side, side), 0), iota((side, side), 1)
    perm[...] = jnp.where(i1 == (i0 & 15) * HW + (i0 >> 4), 1.0, 0.0).astype(BF)

    def turn(block):
        return dot(perm[...], block.reshape(side, chans)).astype(BF).reshape(HW, HW, chans)

    def stage(field, raw, ext):
        raw[pl.ds(cols, own - cols)] = jnp.zeros((own - cols, rows, chans), BF)
        tails[field] = turn(raw[pl.ds(cols - HW, HW)])
        for b in range(own // HW):
            ext[pl.ds(1, rows), pl.ds(b * HW, HW)] = turn(raw[pl.ds(b * HW, HW)])

    def remote(src, dst, snd, rcv, device):
        return pltpu.make_async_remote_copy(
            src_ref=src,
            dst_ref=dst,
            send_sem=snd,
            recv_sem=rcv,
            device_id=device,
            device_id_type=MESH,
        )

    def halo(field, ext, parts=(0, 1)):
        tail = tails.at[field]
        top = rows // 2 + 1
        upper, lower = pl.ds(1, top), pl.ds(1 + top, rows - top)
        moves = [
            [
                (tail.at[pl.ds(0, top)], ext.at[upper, pl.ds(left, HW)], 0),
                (ext.at[upper, pl.ds(0, HW)], ext.at[upper, pl.ds(right, HW)], 1),
                (ext.at[rows, pl.ds(0, own)], ext.at[0, pl.ds(0, own)], 2),
                (tail.at[rows - 1], ext.at[0, pl.ds(left, HW)], 4),
                (ext.at[rows, pl.ds(0, HW)], ext.at[0, pl.ds(right, HW)], 6),
            ],
            [
                (tail.at[pl.ds(top, rows - top)], ext.at[lower, pl.ds(left, HW)], 0),
                (ext.at[lower, pl.ds(0, HW)], ext.at[lower, pl.ds(right, HW)], 1),
                (ext.at[1, pl.ds(0, own)], ext.at[rows + 1, pl.ds(0, own)], 3),
                (tail.at[0], ext.at[rows + 1, pl.ds(left, HW)], 5),
                (ext.at[1, pl.ds(0, HW)], ext.at[rows + 1, pl.ds(right, HW)], 7),
            ],
        ]
        return [
            remote(src, dst, halo_snd.at[field, part, i], halo_rcv.at[field, part, i], around[to])
            for part in parts
            for i, (src, dst, to) in enumerate(moves[part])
        ]

    def tap_copies():
        return [
            remote(edge_out.at[i], edge_in.at[i], tap_snd.at[i], tap_rcv.at[i], device)
            for i, device in enumerate([(south, lon), (north, lon)])
        ]

    def start(copies):
        for copy in copies:
            copy.start()

    def arrive(copies):
        for copy in copies:
            copy.wait_recv()

    def sent(copies):
        for copy in copies:
            copy.wait_send()

    inputs[0].wait()
    stage(0, raw_f, ext_f)
    pl.semaphore_wait(barrier, len(around) + len(others))
    start(halo(0, ext_f))

    loose[...] = jnp.zeros(loose.shape, F32)
    row = iota((rows, WIDE), 0)
    lane = iota((rows, WIDE), 1)
    reach = jnp.zeros((rows, WIDE), jnp.int32)
    for r in range(rows):
        reach = jnp.where(row == r, support_ref[r], reach)
    inside = jnp.abs(lane - HW) <= reach
    for k in range(basis):
        for a in range(3):
            loose[k * 3 + a, :, pl.ds(0, SPAN)] = basis_ref[k, a].astype(F32)
    b0, b1 = iota((WIDE, 2 * WIDE), 0), iota((WIDE, 2 * WIDE), 1)
    place = (b1 == ((b0 - HW) & (WIDE - 1))) | (b1 == ((HW - b0) & (WIDE - 1)) + WIDE)
    place = jnp.where(place, 1.0, 0.0).astype(BF)
    for k in range(basis):
        for a in range(3):
            ka = k * 3 + a
            masked = jnp.where(inside, loose[ka], 0.0).astype(BF)
            placed = dot(masked, place)
            edge_out[0, pl.ds(ka, 1)] = placed[rows - 1 : rows, WIDE:]
            edge_out[1, pl.ds(ka, 1)] = placed[:1, WIDE:]
            forward = placed[:, :WIDE]
            if a == 0:
                forward = jnp.where((row == 0) & (lat == 0), 0.0, forward)
            elif a == 2:
                forward = jnp.where((row == rows - 1) & (lat == nlat - 1), 0.0, forward)
            for r in range(rows):
                taps[r, pl.ds(ka, 1), pl.ds(0, WIDE)] = forward[r : r + 1]
                taps[r, pl.ds(ka, 1), pl.ds(WIDE, WIDE)] = placed[r : r + 1, WIDE:]
    start(tap_copies())

    low_tiles = [own - 2 * HW, own - HW]
    at = iota((HW, WIDE), 1)
    plain, moved = [], []
    for j in low_tiles:
        valid = iota((HW, WIDE), 0) + j < cols
        plain.append(valid & ((at < cols) | (at >= left)))
        moved.append(valid & (at >= right) & (at < left))
    gap = own - cols

    def toeplitz(tap):
        wide = jnp.broadcast_to(tap, (HW, WIDE))
        tile = pltpu.roll(wide, 0, 1, stride=1, stride_axis=0).astype(BF)
        tiles = [tile] + [pltpu.roll(tile, j, 1) for j in range(HW, own, HW)]
        for i, j in enumerate(low_tiles):
            shifted = pltpu.roll(tile, j + gap, 1)
            tiles[j // HW] = jnp.where(moved[i], shifted, jnp.where(plain[i], tiles[j // HW], 0))
        return jnp.concatenate(tiles, axis=0)

    def build_fwd(r, carry):
        for k in range(basis):
            for a in range(3):
                tap = taps[r, pl.ds(k * 3 + a, 1), pl.ds(0, WIDE)]
                band[r, pl.ds(k * own, own), pl.ds(a * WIDE, WIDE)] = toeplitz(tap)
        return carry

    def build_back(r, carry):
        for k in range(basis):
            for a in range(3):
                tap = taps[r, pl.ds(k * 3 + a, 1), pl.ds(WIDE, WIDE)]
                t = 2 - a
                back[r + a, pl.ds(k * own, own), pl.ds(t * WIDE, WIDE)] = toeplitz(tap)
        return carry

    lax.fori_loop(0, rows, build_fwd, 0)

    inputs[1].wait()
    stage(1, raw_c, ext_c)
    inputs[2].wait()
    inputs[3].wait()
    eye = jnp.where(iota((chans, chans), 0) == iota((chans, chans), 1), 1.0, 0.0).astype(BF)
    for k in range(basis):
        w1t[k] = dot(eye, w1[k], NT).astype(BF)
        w2t[k] = dot(eye, w2[k], NT).astype(BF)
    lax.fori_loop(0, rows, build_back, 0)

    def stencil(ext, matrix, at, y, r):
        x = ext[pl.ds(r, 3)].reshape(3 * WIDE, chans)
        t = dot(matrix[r + at], x).astype(BF)
        for k in range(basis):
            y[r, :, pl.ds(k * chans, chans)] = t[k * own : (k + 1) * own]

    def convolve(ext, matrix, at, y, w, r0):
        for i in range(blk):
            stencil(ext, matrix, at, y, r0 + i)
        flat = y[pl.ds(r0, blk)].reshape(blk * own, wide_chans)
        return dot(flat, w[...].reshape(wide_chans, chans))

    def put(field, ext, r0, value):
        value = value.reshape(blk, own, chans)
        ext[pl.ds(r0 + 1, blk), pl.ds(0, own)] = value.astype(BF)
        for i in range(blk):
            tails[field, r0 + i] = value[i, cols - HW : cols].astype(BF)

    def first(b, carry):
        r0 = b * blk
        z = convolve(ext_f, band, 0, y1, w1, r0)
        sigma = jax.nn.sigmoid(z)
        dsig[pl.ds(r0, blk)] = (sigma * (1.0 + z * (1.0 - sigma))).reshape(blk, own, chans)
        put(2, ext_h, r0, z * sigma)
        return carry

    def first_back(b, carry):
        r0 = b * blk
        g = convolve(ext_c, back, 1, v2, w2t, r0)
        put(3, ext_d, r0, g * dsig[pl.ds(r0, blk)].reshape(blk * own, chans))
        return carry

    def second(b, carry):
        r0 = b * blk
        z = convolve(ext_h, band, 0, tmp, w2, r0)
        natural[0, pl.ds(r0, blk)] = z.astype(BF).reshape(blk, own, chans)
        return carry

    def second_back(b, carry):
        r0 = b * blk
        z = convolve(ext_d, back, 1, tmp, w1t, r0)
        natural[1, pl.ds(r0, blk)] = z.astype(BF).reshape(blk, own, chans)
        return carry

    def outgoing(i, ref):
        return pltpu.make_async_copy(turned.at[i, pl.ds(0, cols)], ref, out_sem.at[i])

    def emit(i, ref):
        for b in range(own // HW):
            turned[i, pl.ds(b * HW, HW)] = turn(natural[i, :, pl.ds(b * HW, HW)])
        outgoing(i, ref).start()

    chunk = wide_chans // nx
    half = chunk // 2
    slab = chunk // ny
    far_first = sorted(range(nx), key=lambda d: -min(d, nx - d))
    near_first = far_first[::-1]
    far_first_y = sorted(range(ny), key=lambda d: -min(d, ny - d))

    def core_scatter(d):
        x = x_peers[d]
        return remote(gb.at[x], r1.at[x], core_snd.at[0, d], core_rcv.at[0, d], partner)

    def xy_scatter(dx, dy):
        i = dx * ny + dy
        src = sb.at[x_peers[dx], y_peers[dy]]
        return remote(src, r2.at[i], xy_snd.at[0, i], xy_rcv.at[0, i], xy_devices[dx, dy])

    def z_spread(d):
        own_slab = zall.at[my_z]
        return remote(own_slab, own_slab, z_snd.at[d], z_rcv.at[d], z_devices[d])

    def xy_gather(dx, dy):
        i = dx * ny + dy
        own_slab = gfull.at[my_core, my_x, my_y]
        return remote(own_slab, own_slab, xy_snd.at[1, i], xy_rcv.at[1, i], xy_devices[dx, dy])

    def core_gather(d):
        arrived = gfull.at[my_core, x_from[d]]
        return remote(arrived, arrived, core_snd.at[1, d], core_rcv.at[1, d], partner)

    xy_order = [(dx, dy) for dx in far_first for dy in far_first_y if dx + dy > 0]

    def keep_grad(g, value, first):
        for core in range(2):
            for x in range(nx):
                at = (core * nx + x) * half
                to = (core, x, pl.ds(g * half, half))
                share = value[at : at + half]
                p32[to] = share if first else p32[to] + share

    def reduce_core():
        for dx in far_first:
            x = x_peers[dx]
            core_scatter(dx).wait_recv()
            total = p32[my_core, x].reshape(ny, slab, chans) + r1[x].astype(F32)
            sb[x] = total.astype(BF)
            start([xy_scatter(*to) for to in xy_order if to[0] == dx])

    def reduce_xy():
        total = p32[my_core, my_x, pl.ds(pl.multiple_of(my_y * slab, slab), slab)]
        total = total + r1[my_x, my_y].astype(F32)
        for to in xy_order[::-1]:
            xy_scatter(*to).wait_recv()
            total = total + r2[to[0] * ny + to[1]].astype(F32)
        zall[my_z] = total.astype(BF)
        start([z_spread(d) for d in sorted(range(1, nz), key=lambda d: -min(d, nz - d))])

    def reduce_z():
        arrive([z_spread(d) for d in range(1, nz)])
        total = zall[0].astype(F32)
        for z in range(1, nz):
            total = total + zall[z].astype(F32)
        gfull[my_core, my_x, my_y] = (total * scaling).astype(BF)
        start([xy_gather(*to) for to in xy_order])

    def gather_xy():
        for dx in near_first:
            arrive([xy_gather(*to) for to in xy_order if to[0] == dx])
            core_gather(dx).start()

    def gather_core():
        arrive([core_gather(d) for d in range(nx)])

    def mine(ext, r0, count):
        return ext[pl.ds(r0 + 1, count), pl.ds(0, own)].reshape(count * own, chans)

    def weight_grads(r0, count, first):
        flat = v2[pl.ds(r0, count)].reshape(count * own, wide_chans)
        grad = dot(mine(ext_h, r0, count), flat, TN)
        parts = [grad[:, k * chans : (k + 1) * chans] for k in range(basis)]
        keep_grad(1, jnp.concatenate(parts, 0), first)
        flat = y1[pl.ds(r0, count)].reshape(count * own, wide_chans)
        keep_grad(0, dot(flat, mine(ext_d, r0, count), TN), first)

    def halves(field, ext, body, between=None):
        for part in range(2):
            arrive(halo(field, ext, (part,)))
            lax.fori_loop(part * nblk // 2, (part + 1) * nblk // 2, body, 0)
            if between is not None:
                between(part)

    sent(halo(0, ext_f))
    start(halo(1, ext_c))
    halves(0, ext_f, first)
    sent(halo(1, ext_c))
    start(halo(2, ext_h))

    arrive(tap_copies())
    for k in range(basis):
        tap = jnp.where(lat > 0, edge_in[0, pl.ds(k * 3 + 2, 1)], 0.0)
        back[1, pl.ds(k * own, own), pl.ds(0, WIDE)] = toeplitz(tap)
        tap = jnp.where(lat < nlat - 1, edge_in[1, pl.ds(k * 3, 1)], 0.0)
        back[rows, pl.ds(k * own, own), pl.ds(2 * WIDE, WIDE)] = toeplitz(tap)
    halves(
        1,
        ext_c,
        first_back,
        lambda part: weight_grads(part * (rows // 2), rows // 2, part == 0),
    )
    gb[...] = p32[1 - my_core].astype(BF).reshape(gb.shape)
    start([core_scatter(d) for d in far_first])
    reduce_core()
    halves(2, ext_h, second)
    reduce_xy()
    sent(halo(2, ext_h))
    start(halo(3, ext_d))
    emit(0, out_ref)
    reduce_z()
    halves(3, ext_d, second_back)
    emit(1, gin_ref)
    gather_xy()
    gather_core()
    last = pltpu.make_async_copy(gfull, grad_ref, out_sem.at[2])
    last.start()

    sent(halo(3, ext_d) + tap_copies())
    sent([make(d) for make in (core_scatter, core_gather) for d in range(nx)])
    sent([make(*to) for make in (xy_scatter, xy_gather) for to in xy_order])
    sent([z_spread(d) for d in range(1, nz)])
    outgoing(0, out_ref).wait()
    outgoing(1, gin_ref).wait()
    last.wait()


def deliver(nx, half, out_in, gin_in, grad_in, out_ref, gin_ref, g1_ref, g2_ref, grad, g1, g2, sems):
    def put(i, src, dst):
        return pltpu.make_async_copy(src, dst, sems.at[i])

    arriving = put(4, grad_in, grad)
    arriving.start()
    leaving = [put(0, out_in, out_ref), put(1, gin_in, gin_ref)]
    for copy in leaving:
        copy.start()
    arriving.wait()
    for core in range(2):
        for x in range(nx):
            at = pl.ds((core * nx + x) * half, half)
            flat = grad[core, x].reshape(2 * half, grad.shape[-1]).astype(F32)
            g1[at] = flat[:half]
            g2[at] = flat[half:]
    leaving += [put(2, g1, g1_ref), put(3, g2, g2_ref)]
    for copy in leaving[2:]:
        copy.start()
    for copy in leaving:
        copy.wait()


def local(sizes, features, cotangent, basis, support, weight_one, weight_two):
    nx, nyl, nz, nyh = sizes
    rows, cols, chans = features.shape
    count = weight_one.shape[0]
    nlat, nlon = nx * nyl * 2, nz * nyh
    ny = nyl * nyh
    scaling = 1.0 / math.sqrt(rows * nlat * cols * nlon)
    own = -(-cols // 16) * 16
    chunk = count * chans // nx
    slab = chunk // ny

    vmem = pl.BlockSpec(memory_space=pltpu.VMEM)
    smem = pl.BlockSpec(memory_space=pltpu.SMEM)
    hbm = pl.BlockSpec(memory_space=pl.ANY)
    dma = pltpu.SemaphoreType.DMA
    ext = pltpu.VMEM((rows + 2, WIDE, chans), BF)
    field = jax.ShapeDtypeStruct((cols, rows, chans), BF)
    out, gin, grads = pl.pallas_call(
        functools.partial(kernel, (nx, nyl, nz, nyh, rows, cols, chans, count, scaling)),
        out_shape=(
            pltpu.VMEM((cols, rows, chans), BF),
            pltpu.VMEM((cols, rows, chans), BF),
            pltpu.VMEM((2, nx, ny, slab, chans), BF),
        ),
        in_specs=[hbm, hbm, vmem, smem, hbm, hbm],
        out_specs=(hbm,) * 3,
        scratch_shapes=[
            pltpu.VMEM((own, rows, chans), BF),
            pltpu.VMEM((own, rows, chans), BF),
            pltpu.VMEM((count, chans, chans), BF),
            pltpu.VMEM((count, chans, chans), BF),
            pltpu.VMEM((count, chans, chans), BF),
            pltpu.VMEM((count, chans, chans), BF),
            pltpu.VMEM((HW * HW, HW * HW), BF),
            ext,
            ext,
            ext,
            ext,
            pltpu.VMEM((4, rows, HW, chans), BF),
            pltpu.VMEM((count * 3, rows, WIDE), F32),
            pltpu.VMEM((rows, count * 3, 2 * WIDE), F32),
            pltpu.VMEM((2, count * 3, WIDE), F32),
            pltpu.VMEM((2, count * 3, WIDE), F32),
            pltpu.VMEM((rows, count * own, 3 * WIDE), BF),
            pltpu.VMEM((rows + 2, count * own, 3 * WIDE), BF),
            pltpu.VMEM((rows, own, count * chans), BF),
            pltpu.VMEM((rows, own, count * chans), BF),
            pltpu.VMEM((rows, own, count * chans), BF),
            pltpu.VMEM((rows, own, chans), F32),
            pltpu.VMEM((2, rows, own, chans), BF),
            pltpu.VMEM((2, own, rows, chans), BF),
            pltpu.VMEM((2, nx, chunk, chans), F32),
            pltpu.VMEM((nx, ny, slab, chans), BF),
            pltpu.VMEM((nx, ny, slab, chans), BF),
            pltpu.VMEM((nx, ny, slab, chans), BF),
            pltpu.VMEM((nx * ny, slab, chans), BF),
            pltpu.VMEM((nz, slab, chans), BF),
            pltpu.VMEM((2, nx, ny, slab, chans), BF),
            dma((4,)),
            dma((3,)),
            dma((4, 2, 5)),
            dma((4, 2, 5)),
            dma((2,)),
            dma((2,)),
            dma((2, nx)),
            dma((2, nx)),
            dma((2, nx * ny)),
            dma((2, nx * ny)),
            dma((nz,)),
            dma((nz,)),
        ],
        compiler_params=pltpu.CompilerParams(
            collective_id=0, has_side_effects=True, vmem_limit_bytes=58 * 1024 * 1024
        ),
    )(
        features.transpose(1, 0, 2),
        cotangent.transpose(1, 0, 2),
        basis.transpose(1, 2, 0, 3),
        support,
        weight_one,
        weight_two,
    )
    weights = jax.ShapeDtypeStruct((count * chans, chans), F32)
    out, gin, g1, g2 = pl.pallas_call(
        functools.partial(deliver, nx, chunk // 2),
        out_shape=(field, field, weights, weights),
        in_specs=[hbm] * 3,
        out_specs=(hbm,) * 4,
        scratch_shapes=[
            pltpu.VMEM(grads.shape, BF),
            pltpu.VMEM(weights.shape, F32),
            pltpu.VMEM(weights.shape, F32),
            dma((5,)),
        ],
        compiler_params=pltpu.CompilerParams(vmem_limit_bytes=8 * 1024 * 1024),
    )(out, gin, grads)
    shape = weight_one.shape
    return out.transpose(1, 0, 2), gin.transpose(1, 0, 2), g1.reshape(shape), g2.reshape(shape)


def solution(mesh):
    nlat, nlon = mesh.shape["lat"], mesh.shape["lon"]
    nyl = 2 if nlat >= 16 else 1
    sizes = (nlat // (2 * nyl), nyl, nlon // 2, 2)
    placed = (
        P("lat", "lon", None),
        P("lat", "lon", None),
        P("lat", None, None, None),
        P("lat"),
        P(),
        P(),
    )
    return jax.shard_map(
        functools.partial(local, sizes),
        mesh=mesh,
        in_specs=placed,
        out_specs=(P("lat", "lon", None), P("lat", "lon", None), P(), P()),
        check_vma=False,
    )
```

```python
import functools
import math

import jax
import jax.numpy as jnp
from jax import lax
from jax.experimental import pallas as pl
from jax.experimental.pallas import tpu as pltpu
from jax.sharding import PartitionSpec as P

HW = 16
SPAN = 2 * HW + 1
WIDE = 128
MESH = pl.DeviceIdType.MESH
BF = jnp.bfloat16
F32 = jnp.float32
NN = (((1,), (0,)), ((), ()))
NT = (((1,), (1,)), ((), ()))
TN = (((0,), (0,)), ((), ()))


def dot(a, b, dims=NN):
    return lax.dot_general(a, b, dims, preferred_element_type=F32)


def iota(shape, dim):
    return lax.broadcasted_iota(jnp.int32, shape, dim)


def kernel(
    dims,
    f_ref,
    c_ref,
    basis_ref,
    support_ref,
    w1_ref,
    w2_ref,
    out_ref,
    gin_ref,
    grad_ref,
    raw_f,
    raw_c,
    w1,
    w2,
    w1t,
    w2t,
    perm,
    ext_f,
    ext_c,
    ext_h,
    ext_d,
    tails,
    loose,
    taps,
    edge_out,
    edge_in,
    band,
    back,
    y1,
    v2,
    tmp,
    dsig,
    natural,
    turned,
    p32,
    gb,
    r1,
    sb,
    r2,
    zall,
    gfull,
    in_sem,
    out_sem,
    halo_snd,
    halo_rcv,
    tap_snd,
    tap_rcv,
    core_snd,
    core_rcv,
    xy_snd,
    xy_rcv,
    z_snd,
    z_rcv,
):
    nx, nyl, nz, nyh, rows, cols, chans, basis, scaling = dims
    own = -(-cols // 16) * 16
    right = own
    left = WIDE - HW
    nlat, nlon = nx * nyl * 2, nz * nyh
    ny = nyl * nyh
    blk = 8
    nblk = rows // blk
    wide_chans = basis * chans

    inputs = [
        pltpu.make_async_copy(src, dst, in_sem.at[i])
        for i, (src, dst) in enumerate(
            [
                (f_ref, raw_f.at[pl.ds(0, cols)]),
                (c_ref, raw_c.at[pl.ds(0, cols)]),
                (w1_ref, w1),
                (w2_ref, w2),
            ]
        )
    ]
    for copy in inputs:
        copy.start()

    lat = lax.axis_index("lat")
    lon = lax.axis_index("lon")

    def wrap(value, count):
        return jnp.where(value >= count, value - count, value)

    my_x = lat // (nyl * 2)
    in_x = lat - my_x * (nyl * 2)
    my_yl = in_x // 2
    my_core = in_x - my_yl * 2
    my_z = lon // nyh
    my_y = (lon - my_z * nyh) * nyl + my_yl
    north, south = wrap(lat + nlat - 1, nlat), wrap(lat + 1, nlat)
    west, east = wrap(lon + nlon - 1, nlon), wrap(lon + 1, nlon)

    partner = (lat + 1 - 2 * my_core, lon)
    around = [
        (lat, east),
        (lat, west),
        (south, lon),
        (north, lon),
        (south, east),
        (north, east),
        (south, west),
        (north, west),
    ]
    x_peers = [wrap(my_x + d, nx) for d in range(nx)]
    x_from = [wrap(my_x + nx - d, nx) for d in range(nx)]
    y_peers = [wrap(my_y + d, ny) for d in range(ny)]
    z_peers = [wrap(my_z + d, nz) for d in range(nz)]
    my_yh = lon - my_z * nyh
    xy_devices = {}
    for dy, y in enumerate(y_peers):
        yh = y // nyl
        for dx, x in enumerate(x_peers):
            to = (x * (nyl * 2) + (y - yh * nyl) * 2 + my_core, my_z * nyh + yh)
            xy_devices[dx, dy] = to
    z_devices = [(lat, z * nyh + my_yh) for z in z_peers]

    barrier = pltpu.get_barrier_semaphore()

    def greet(device):
        pl.semaphore_signal(barrier, inc=1, device_id=device, device_id_type=MESH)

    for device in around:
        greet(device)
    others = z_devices[1:] + list(xy_devices.values())[1:] + [partner]
    for device in others:
        greet(device)

    side = HW * HW
    i0, i1 = iota((side, side), 0), iota((side, side), 1)
    perm[...] = jnp.where(i1 == (i0 & 15) * HW + (i0 >> 4), 1.0, 0.0).astype(BF)

    def turn(block):
        return dot(perm[...], block.reshape(side, chans)).astype(BF).reshape(HW, HW, chans)

    def stage_ends(field, raw, ext):
        tails[field] = turn(raw[pl.ds(cols - HW, HW)])
        ext[pl.ds(1, rows), pl.ds(0, HW)] = turn(raw[pl.ds(0, HW)])

    def stage_rest(raw, ext):
        raw[pl.ds(cols, own - cols)] = jnp.zeros((own - cols, rows, chans), BF)
        for b in range(1, own // HW):
            ext[pl.ds(1, rows), pl.ds(b * HW, HW)] = turn(raw[pl.ds(b * HW, HW)])

    def remote(src, dst, snd, rcv, device):
        return pltpu.make_async_remote_copy(
            src_ref=src,
            dst_ref=dst,
            send_sem=snd,
            recv_sem=rcv,
            device_id=device,
            device_id_type=MESH,
        )

    def halo(field, ext, parts=(0, 1)):
        tail = tails.at[field]
        top = rows // 2 + 1
        upper, lower = pl.ds(1, top), pl.ds(1 + top, rows - top)
        moves = [
            [
                (tail.at[pl.ds(0, top)], ext.at[upper, pl.ds(left, HW)], 0),
                (ext.at[upper, pl.ds(0, HW)], ext.at[upper, pl.ds(right, HW)], 1),
                (ext.at[rows, pl.ds(0, own)], ext.at[0, pl.ds(0, own)], 2),
                (tail.at[rows - 1], ext.at[0, pl.ds(left, HW)], 4),
                (ext.at[rows, pl.ds(0, HW)], ext.at[0, pl.ds(right, HW)], 6),
            ],
            [
                (tail.at[pl.ds(top, rows - top)], ext.at[lower, pl.ds(left, HW)], 0),
                (ext.at[lower, pl.ds(0, HW)], ext.at[lower, pl.ds(right, HW)], 1),
                (ext.at[1, pl.ds(0, own)], ext.at[rows + 1, pl.ds(0, own)], 3),
                (tail.at[0], ext.at[rows + 1, pl.ds(left, HW)], 5),
                (ext.at[1, pl.ds(0, HW)], ext.at[rows + 1, pl.ds(right, HW)], 7),
            ],
        ]
        return [
            remote(src, dst, halo_snd.at[field, part, i], halo_rcv.at[field, part, i], around[to])
            for part in parts
            for i, (src, dst, to) in enumerate(moves[part])
        ]

    def tap_copies():
        return [
            remote(edge_out.at[i], edge_in.at[i], tap_snd.at[i], tap_rcv.at[i], device)
            for i, device in enumerate([(south, lon), (north, lon)])
        ]

    def start(copies):
        for copy in copies:
            copy.start()

    def arrive(copies):
        for copy in copies:
            copy.wait_recv()

    def sent(copies):
        for copy in copies:
            copy.wait_send()

    inputs[0].wait()
    stage_ends(0, raw_f, ext_f)
    pl.semaphore_wait(barrier, len(around) + len(others))
    margins = halo(0, ext_f)
    whole_rows = margins[2::5]
    start([copy for i, copy in enumerate(margins) if i % 5 != 2])
    stage_rest(raw_f, ext_f)
    start(whole_rows)

    loose[...] = jnp.zeros(loose.shape, F32)
    row = iota((rows, WIDE), 0)
    lane = iota((rows, WIDE), 1)
    reach = jnp.zeros((rows, WIDE), jnp.int32)
    for r in range(rows):
        reach = jnp.where(row == r, support_ref[r], reach)
    inside = jnp.abs(lane - HW) <= reach
    for k in range(basis):
        for a in range(3):
            loose[k * 3 + a, :, pl.ds(0, SPAN)] = basis_ref[k, a].astype(F32)
    b0, b1 = iota((WIDE, 2 * WIDE), 0), iota((WIDE, 2 * WIDE), 1)
    place = (b1 == ((b0 - HW) & (WIDE - 1))) | (b1 == ((HW - b0) & (WIDE - 1)) + WIDE)
    place = jnp.where(place, 1.0, 0.0).astype(BF)
    for k in range(basis):
        for a in range(3):
            ka = k * 3 + a
            masked = jnp.where(inside, loose[ka], 0.0).astype(BF)
            placed = dot(masked, place)
            edge_out[0, pl.ds(ka, 1)] = placed[rows - 1 : rows, WIDE:]
            edge_out[1, pl.ds(ka, 1)] = placed[:1, WIDE:]
            forward = placed[:, :WIDE]
            if a == 0:
                forward = jnp.where((row == 0) & (lat == 0), 0.0, forward)
            elif a == 2:
                forward = jnp.where((row == rows - 1) & (lat == nlat - 1), 0.0, forward)
            for r in range(rows):
                taps[r, pl.ds(ka, 1), pl.ds(0, WIDE)] = forward[r : r + 1]
                taps[r, pl.ds(ka, 1), pl.ds(WIDE, WIDE)] = placed[r : r + 1, WIDE:]
    start(tap_copies())

    low_tiles = [own - 2 * HW, own - HW]
    at = iota((HW, WIDE), 1)
    plain, moved = [], []
    for j in low_tiles:
        valid = iota((HW, WIDE), 0) + j < cols
        plain.append(valid & ((at < cols) | (at >= left)))
        moved.append(valid & (at >= right) & (at < left))
    gap = own - cols

    def toeplitz(tap):
        wide = jnp.broadcast_to(tap, (HW, WIDE))
        tile = pltpu.roll(wide, 0, 1, stride=1, stride_axis=0).astype(BF)
        tiles = [tile] + [pltpu.roll(tile, j, 1) for j in range(HW, own, HW)]
        for i, j in enumerate(low_tiles):
            shifted = pltpu.roll(tile, j + gap, 1)
            tiles[j // HW] = jnp.where(moved[i], shifted, jnp.where(plain[i], tiles[j // HW], 0))
        return jnp.concatenate(tiles, axis=0)

    def build_fwd(r, carry):
        for k in range(basis):
            for a in range(3):
                tap = taps[r, pl.ds(k * 3 + a, 1), pl.ds(0, WIDE)]
                band[r, pl.ds(k * own, own), pl.ds(a * WIDE, WIDE)] = toeplitz(tap)
        return carry

    def build_back(r, carry):
        for k in range(basis):
            for a in range(3):
                tap = taps[r, pl.ds(k * 3 + a, 1), pl.ds(WIDE, WIDE)]
                t = 2 - a
                back[r + a, pl.ds(k * own, own), pl.ds(t * WIDE, WIDE)] = toeplitz(tap)
        return carry

    lax.fori_loop(0, rows, build_fwd, 0)

    inputs[1].wait()
    stage_ends(1, raw_c, ext_c)
    stage_rest(raw_c, ext_c)
    inputs[2].wait()
    inputs[3].wait()
    eye = jnp.where(iota((chans, chans), 0) == iota((chans, chans), 1), 1.0, 0.0).astype(BF)
    for k in range(basis):
        w1t[k] = dot(eye, w1[k], NT).astype(BF)
        w2t[k] = dot(eye, w2[k], NT).astype(BF)
    lax.fori_loop(0, rows, build_back, 0)

    def stencil(ext, matrix, at, y, r):
        x = ext[pl.ds(r, 3)].reshape(3 * WIDE, chans)
        t = dot(matrix[r + at], x).astype(BF)
        for k in range(basis):
            y[r, :, pl.ds(k * chans, chans)] = t[k * own : (k + 1) * own]

    def convolve(ext, matrix, at, y, w, r0):
        for i in range(blk):
            stencil(ext, matrix, at, y, r0 + i)
        flat = y[pl.ds(r0, blk)].reshape(blk * own, wide_chans)
        return dot(flat, w[...].reshape(wide_chans, chans))

    def put(field, ext, r0, value):
        value = value.reshape(blk, own, chans)
        ext[pl.ds(r0 + 1, blk), pl.ds(0, own)] = value.astype(BF)
        for i in range(blk):
            tails[field, r0 + i] = value[i, cols - HW : cols].astype(BF)

    def first(b, carry):
        r0 = b * blk
        z = convolve(ext_f, band, 0, y1, w1, r0)
        sigma = jax.nn.sigmoid(z)
        dsig[pl.ds(r0, blk)] = (sigma * (1.0 + z * (1.0 - sigma))).reshape(blk, own, chans)
        put(2, ext_h, r0, z * sigma)
        return carry

    def first_back(b, carry):
        r0 = b * blk
        g = convolve(ext_c, back, 1, v2, w2t, r0)
        put(3, ext_d, r0, g * dsig[pl.ds(r0, blk)].reshape(blk * own, chans))
        return carry

    def second(b, carry):
        r0 = b * blk
        z = convolve(ext_h, band, 0, tmp, w2, r0)
        natural[0, pl.ds(r0, blk)] = z.astype(BF).reshape(blk, own, chans)
        return carry

    def second_back(b, carry):
        r0 = b * blk
        z = convolve(ext_d, back, 1, tmp, w1t, r0)
        natural[1, pl.ds(r0, blk)] = z.astype(BF).reshape(blk, own, chans)
        return carry

    def outgoing(i, ref):
        return pltpu.make_async_copy(turned.at[i, pl.ds(0, cols)], ref, out_sem.at[i])

    def emit(i, ref):
        for b in range(own // HW):
            turned[i, pl.ds(b * HW, HW)] = turn(natural[i, :, pl.ds(b * HW, HW)])
        outgoing(i, ref).start()

    chunk = wide_chans // nx
    half = chunk // 2
    slab = chunk // ny
    far_first = sorted(range(nx), key=lambda d: -min(d, nx - d))
    near_first = far_first[::-1]
    far_first_y = sorted(range(ny), key=lambda d: -min(d, ny - d))

    def core_scatter(d):
        x = x_peers[d]
        return remote(gb.at[x], r1.at[x], core_snd.at[0, d], core_rcv.at[0, d], partner)

    def xy_scatter(dx, dy):
        i = dx * ny + dy
        src = sb.at[x_peers[dx], y_peers[dy]]
        return remote(src, r2.at[i], xy_snd.at[0, i], xy_rcv.at[0, i], xy_devices[dx, dy])

    def z_spread(d):
        own_slab = zall.at[my_z]
        return remote(own_slab, own_slab, z_snd.at[d], z_rcv.at[d], z_devices[d])

    def xy_gather(dx, dy):
        i = dx * ny + dy
        own_slab = gfull.at[my_core, my_x, my_y]
        return remote(own_slab, own_slab, xy_snd.at[1, i], xy_rcv.at[1, i], xy_devices[dx, dy])

    def core_gather(d):
        arrived = gfull.at[my_core, x_from[d]]
        return remote(arrived, arrived, core_snd.at[1, d], core_rcv.at[1, d], partner)

    xy_order = [(dx, dy) for dx in far_first for dy in far_first_y if dx + dy > 0]

    def keep_grad(g, value, first):
        for core in range(2):
            for x in range(nx):
                at = (core * nx + x) * half
                to = (core, x, pl.ds(g * half, half))
                share = value[at : at + half]
                p32[to] = share if first else p32[to] + share

    def reduce_core():
        for dx in far_first:
            x = x_peers[dx]
            core_scatter(dx).wait_recv()
            total = p32[my_core, x].reshape(ny, slab, chans) + r1[x].astype(F32)
            sb[x] = total.astype(BF)
            start([xy_scatter(*to) for to in xy_order if to[0] == dx])

    def reduce_xy():
        total = p32[my_core, my_x, pl.ds(pl.multiple_of(my_y * slab, slab), slab)]
        total = total + r1[my_x, my_y].astype(F32)
        for to in xy_order[::-1]:
            xy_scatter(*to).wait_recv()
            total = total + r2[to[0] * ny + to[1]].astype(F32)
        zall[my_z] = total.astype(BF)
        start([z_spread(d) for d in sorted(range(1, nz), key=lambda d: -min(d, nz - d))])

    def reduce_z():
        arrive([z_spread(d) for d in range(1, nz)])
        total = zall[0].astype(F32)
        for z in range(1, nz):
            total = total + zall[z].astype(F32)
        gfull[my_core, my_x, my_y] = (total * scaling).astype(BF)
        start([xy_gather(*to) for to in xy_order])

    def gather_xy():
        for dx in near_first:
            arrive([xy_gather(*to) for to in xy_order if to[0] == dx])
            core_gather(dx).start()

    def gather_core():
        arrive([core_gather(d) for d in range(nx)])

    def mine(ext, r0, count):
        return ext[pl.ds(r0 + 1, count), pl.ds(0, own)].reshape(count * own, chans)

    def weight_grads(r0, count, first):
        flat = v2[pl.ds(r0, count)].reshape(count * own, wide_chans)
        grad = dot(mine(ext_h, r0, count), flat, TN)
        parts = [grad[:, k * chans : (k + 1) * chans] for k in range(basis)]
        keep_grad(1, jnp.concatenate(parts, 0), first)
        flat = y1[pl.ds(r0, count)].reshape(count * own, wide_chans)
        keep_grad(0, dot(flat, mine(ext_d, r0, count), TN), first)

    def halves(field, ext, body, between=None):
        for part in range(2):
            arrive(halo(field, ext, (part,)))
            lax.fori_loop(part * nblk // 2, (part + 1) * nblk // 2, body, 0)
            if between is not None:
                between(part)

    sent(halo(0, ext_f))
    start(halo(1, ext_c))
    halves(0, ext_f, first)
    sent(halo(1, ext_c))
    start(halo(2, ext_h))

    arrive(tap_copies())
    for k in range(basis):
        tap = jnp.where(lat > 0, edge_in[0, pl.ds(k * 3 + 2, 1)], 0.0)
        back[1, pl.ds(k * own, own), pl.ds(0, WIDE)] = toeplitz(tap)
        tap = jnp.where(lat < nlat - 1, edge_in[1, pl.ds(k * 3, 1)], 0.0)
        back[rows, pl.ds(k * own, own), pl.ds(2 * WIDE, WIDE)] = toeplitz(tap)
    halves(
        1,
        ext_c,
        first_back,
        lambda part: weight_grads(part * (rows // 2), rows // 2, part == 0),
    )
    for d in far_first:
        x = x_peers[d]
        gb[x] = p32[1 - my_core, x].astype(BF).reshape(ny, slab, chans)
        core_scatter(d).start()
    reduce_core()
    halves(2, ext_h, second)
    reduce_xy()
    sent(halo(2, ext_h))
    start(halo(3, ext_d))
    emit(0, out_ref)
    reduce_z()
    halves(3, ext_d, second_back)
    emit(1, gin_ref)
    gather_xy()
    gather_core()
    last = pltpu.make_async_copy(gfull, grad_ref, out_sem.at[2])
    last.start()

    sent(halo(3, ext_d) + tap_copies())
    sent([make(d) for make in (core_scatter, core_gather) for d in range(nx)])
    sent([make(*to) for make in (xy_scatter, xy_gather) for to in xy_order])
    sent([z_spread(d) for d in range(1, nz)])
    outgoing(0, out_ref).wait()
    outgoing(1, gin_ref).wait()
    last.wait()


def deliver(nx, half, out_in, gin_in, grad_in, out_ref, gin_ref, g1_ref, g2_ref, grad, g1, g2, sems):
    def put(i, src, dst):
        return pltpu.make_async_copy(src, dst, sems.at[i])

    arriving = put(4, grad_in, grad)
    arriving.start()
    leaving = [put(0, out_in, out_ref), put(1, gin_in, gin_ref)]
    for copy in leaving:
        copy.start()
    arriving.wait()
    for core in range(2):
        for x in range(nx):
            at = pl.ds((core * nx + x) * half, half)
            flat = grad[core, x].reshape(2 * half, grad.shape[-1]).astype(F32)
            g1[at] = flat[:half]
            g2[at] = flat[half:]
    leaving += [put(2, g1, g1_ref), put(3, g2, g2_ref)]
    for copy in leaving[2:]:
        copy.start()
    for copy in leaving:
        copy.wait()


def local(sizes, features, cotangent, basis, support, weight_one, weight_two):
    nx, nyl, nz, nyh = sizes
    rows, cols, chans = features.shape
    count = weight_one.shape[0]
    nlat, nlon = nx * nyl * 2, nz * nyh
    ny = nyl * nyh
    scaling = 1.0 / math.sqrt(rows * nlat * cols * nlon)
    own = -(-cols // 16) * 16
    chunk = count * chans // nx
    slab = chunk // ny

    vmem = pl.BlockSpec(memory_space=pltpu.VMEM)
    smem = pl.BlockSpec(memory_space=pltpu.SMEM)
    hbm = pl.BlockSpec(memory_space=pl.ANY)
    dma = pltpu.SemaphoreType.DMA
    ext = pltpu.VMEM((rows + 2, WIDE, chans), BF)
    field = jax.ShapeDtypeStruct((cols, rows, chans), BF)
    out, gin, grads = pl.pallas_call(
        functools.partial(kernel, (nx, nyl, nz, nyh, rows, cols, chans, count, scaling)),
        out_shape=(
            pltpu.VMEM((cols, rows, chans), BF),
            pltpu.VMEM((cols, rows, chans), BF),
            pltpu.VMEM((2, nx, ny, slab, chans), BF),
        ),
        in_specs=[hbm, hbm, vmem, smem, hbm, hbm],
        out_specs=(hbm,) * 3,
        scratch_shapes=[
            pltpu.VMEM((own, rows, chans), BF),
            pltpu.VMEM((own, rows, chans), BF),
            pltpu.VMEM((count, chans, chans), BF),
            pltpu.VMEM((count, chans, chans), BF),
            pltpu.VMEM((count, chans, chans), BF),
            pltpu.VMEM((count, chans, chans), BF),
            pltpu.VMEM((HW * HW, HW * HW), BF),
            ext,
            ext,
            ext,
            ext,
            pltpu.VMEM((4, rows, HW, chans), BF),
            pltpu.VMEM((count * 3, rows, WIDE), F32),
            pltpu.VMEM((rows, count * 3, 2 * WIDE), F32),
            pltpu.VMEM((2, count * 3, WIDE), F32),
            pltpu.VMEM((2, count * 3, WIDE), F32),
            pltpu.VMEM((rows, count * own, 3 * WIDE), BF),
            pltpu.VMEM((rows + 2, count * own, 3 * WIDE), BF),
            pltpu.VMEM((rows, own, count * chans), BF),
            pltpu.VMEM((rows, own, count * chans), BF),
            pltpu.VMEM((rows, own, count * chans), BF),
            pltpu.VMEM((rows, own, chans), F32),
            pltpu.VMEM((2, rows, own, chans), BF),
            pltpu.VMEM((2, own, rows, chans), BF),
            pltpu.VMEM((2, nx, chunk, chans), F32),
            pltpu.VMEM((nx, ny, slab, chans), BF),
            pltpu.VMEM((nx, ny, slab, chans), BF),
            pltpu.VMEM((nx, ny, slab, chans), BF),
            pltpu.VMEM((nx * ny, slab, chans), BF),
            pltpu.VMEM((nz, slab, chans), BF),
            pltpu.VMEM((2, nx, ny, slab, chans), BF),
            dma((4,)),
            dma((3,)),
            dma((4, 2, 5)),
            dma((4, 2, 5)),
            dma((2,)),
            dma((2,)),
            dma((2, nx)),
            dma((2, nx)),
            dma((2, nx * ny)),
            dma((2, nx * ny)),
            dma((nz,)),
            dma((nz,)),
        ],
        compiler_params=pltpu.CompilerParams(
            collective_id=0, has_side_effects=True, vmem_limit_bytes=58 * 1024 * 1024
        ),
    )(
        features.transpose(1, 0, 2),
        cotangent.transpose(1, 0, 2),
        basis.transpose(1, 2, 0, 3),
        support,
        weight_one,
        weight_two,
    )
    weights = jax.ShapeDtypeStruct((count * chans, chans), F32)
    out, gin, g1, g2 = pl.pallas_call(
        functools.partial(deliver, nx, chunk // 2),
        out_shape=(field, field, weights, weights),
        in_specs=[hbm] * 3,
        out_specs=(hbm,) * 4,
        scratch_shapes=[
            pltpu.VMEM(grads.shape, BF),
            pltpu.VMEM(weights.shape, F32),
            pltpu.VMEM(weights.shape, F32),
            dma((5,)),
        ],
        compiler_params=pltpu.CompilerParams(vmem_limit_bytes=8 * 1024 * 1024),
    )(out, gin, grads)
    shape = weight_one.shape
    return out.transpose(1, 0, 2), gin.transpose(1, 0, 2), g1.reshape(shape), g2.reshape(shape)


def solution(mesh):
    nlat, nlon = mesh.shape["lat"], mesh.shape["lon"]
    nyl = 2 if nlat >= 16 else 1
    sizes = (nlat // (2 * nyl), nyl, nlon // 2, 2)
    placed = (
        P("lat", "lon", None),
        P("lat", "lon", None),
        P("lat", None, None, None),
        P("lat"),
        P(),
        P(),
    )
    return jax.shard_map(
        functools.partial(local, sizes),
        mesh=mesh,
        in_specs=placed,
        out_specs=(P("lat", "lon", None), P("lat", "lon", None), P(), P()),
        check_vma=False,
    )
```
